32 devices in a mesh: batch: 8 (over z, core), seq: 4 (over y, x).
Axes of the slice: x: 2, y: 2, z: 4, core: 2. Of those that a mesh axis runs over, the one named last changes fastest.
Arguments:
- inputs: bfloat16 [16, 1024, 2048], P('batch', 'seq'), may hold values from -6 to 6
- cotangent: bfloat16 [16, 1024, 2048], P('batch', 'seq'), may hold values from -6 to 6
- max_exit: int32 [16], P('batch'), may hold values from 5 to 24, as said below
- min_exit: int32 [16], P('batch'), may hold values from 1 to 24
- layer: int32 [1], replicated, may hold values from 4 to 19
- wq: bfloat16 [2048, 2048], P(('batch', 'seq')), may hold values from -0.125 to 0.125
- wk: bfloat16 [2048, 2048], P(('batch', 'seq')), may hold values from -0.125 to 0.125
- wv: bfloat16 [2048, 2048], P(('batch', 'seq')), may hold values from -0.125 to 0.125
- wo: bfloat16 [2048, 2048], P(('batch', 'seq')), may hold values from -0.5 to 0.5
- gain_one: bfloat16 [2048], P(('batch', 'seq')), may hold values from 0.25 to 1.75
- shift_one: bfloat16 [2048], P(('batch', 'seq')), may hold values from -3 to 3
- bias_q: bfloat16 [2048], P(('batch', 'seq')), may hold values from -3 to 3
- bias_v: bfloat16 [2048], P(('batch', 'seq')), may hold values from -3 to 3
- bias_o: bfloat16 [2048], P(('batch', 'seq')), may hold values from -3 to 3
- w_in: bfloat16 [2048, 8192], P(('batch', 'seq')), may hold values from -0.125 to 0.125
- w_out: bfloat16 [8192, 2048], P(('batch', 'seq')), may hold values from -0.09375 to 0.09375
- gain_two: bfloat16 [2048], P(('batch', 'seq')), may hold values from 0.25 to 1.75
- shift_two: bfloat16 [2048], P(('batch', 'seq')), may hold values from -3 to 3
- bias_in: bfloat16 [8192], P(('batch', 'seq')), may hold values from -3 to 3
- bias_out: bfloat16 [2048], P(('batch', 'seq')), may hold values from -3 to 3
Outputs:
- output: bfloat16 [16, 1024, 2048], P('batch', 'seq')
- input_grad: bfloat16 [16, 1024, 2048], P('batch', 'seq')
- query_weight_gradient: float32 [2048, 2048], P(('batch', 'seq'))
- key_weight_gradient: float32 [2048, 2048], P(('batch', 'seq'))
- value_weight_gradient: float32 [2048, 2048], P(('batch', 'seq'))
- output_weight_gradient: float32 [2048, 2048], P(('batch', 'seq'))
- grad_gain_one: float32 [2048], P(('batch', 'seq'))
- grad_shift_one: float32 [2048], P(('batch', 'seq'))
- grad_bias_q: float32 [2048], P(('batch', 'seq'))
- grad_bias_v: float32 [2048], P(('batch', 'seq'))
- grad_bias_o: float32 [2048], P(('batch', 'seq'))
- input_weight_gradient: float32 [2048, 8192], P(('batch', 'seq'))
- grad_w_out: float32 [8192, 2048], P(('batch', 'seq'))
- grad_gain_two: float32 [2048], P(('batch', 'seq'))
- grad_shift_two: float32 [2048], P(('batch', 'seq'))
- grad_bias_in: float32 [8192], P(('batch', 'seq'))
- grad_bias_out: float32 [2048], P(('batch', 'seq'))
The draws below stay inside these ranges and needn't reach their ends.
Inputs may be any that keep to these rules, and one draw needn't show every extreme that they name: Every sequence has max_exit >= min_exit and max_exit > layer[0]; in each of the aligned groups of 2 sequences exactly one has min_exit > layer[0].
All inputs are finite; a program needn't handle non-finite values.
Results may differ from the reference program's by a relative error of at most 0.015.
Values may be sent and summed in bfloat16 or wider, within the bound.
No kernel may reach another device: no remote copies, remote signals or barrier semaphores. Data moves between devices by JAX's collectives and lax.ppermute only.
A program may use at most 448 MiB of HBM per device.

```python
import jax
import jax.numpy as jnp
from jax import lax

D = 2048
HEADS = 32
HEAD_DIM = 64
FF = 8192
N_LAYERS = 24
SEQ_LEN = 1024
SEQS_GRP = 2
SEQS = 16


def exit_plan(key):
    keys_all = jax.random.split(key, 6)
    layer = jax.random.randint(keys_all[0], (1,), 4, N_LAYERS - 4)
    chosen = jax.random.randint(keys_all[1], (SEQS // SEQS_GRP,), 0, SEQS_GRP)
    marked = (jnp.arange(SEQS_GRP)[None, :] == chosen[:, None]).reshape(SEQS)
    places = jnp.arange(SEQS, dtype=jnp.int32)
    deep_low = jax.random.randint(keys_all[2], (SEQS,), layer[0] + 1, N_LAYERS + 1)
    deep_high = jax.random.randint(keys_all[3], (SEQS,), deep_low, N_LAYERS + 1)
    deep_high = jnp.where(places == chosen[0], N_LAYERS, deep_high)
    part_low = jax.random.randint(keys_all[4], (SEQS,), 1, layer[0] + 1)
    part_low = jnp.where(places == (chosen[0] + 1) % SEQS_GRP, 1, part_low)
    part_high = jax.random.randint(keys_all[5], (SEQS,), layer[0] + 1, N_LAYERS + 1)
    highest_exit = jnp.where(marked, deep_high, part_high).astype(jnp.int32)
    lowest_exit = jnp.where(marked, deep_low, part_low).astype(jnp.int32)
    return (layer.astype(jnp.int32), highest_exit, lowest_exit)


def draw_max_exit(key, part):
    planned = exit_plan(key)
    return planned[1]


def draw_min_exit(key, part):
    planned = exit_plan(key)
    return planned[2]


def draw_layer(key, part):
    planned = exit_plan(key)
    return planned[0]


def shard_levels(own_key, shape, pieces, least, top_value):
    loudness = 1.0
    for position, parts in pieces:
        heights = jax.random.uniform(jax.random.fold_in(jax.random.fold_in(own_key, 6), position), (parts,), jnp.float32, least / len(pieces), top_value / len(pieces))
        loudness = loudness * jnp.repeat(jnp.exp(heights), shape[position] // parts).reshape((-1,) + (1,) * (len(shape) - 1 - position))
    return loudness


def centred(stream_key, shape, scale, most, cuts=(), held_as=jnp.bfloat16):
    values = jax.random.normal(stream_key, shape, jnp.float32) * scale
    if len(cuts) > 0:
        values = shard_levels(stream_key, shape, cuts, -0.22, 0.18) * values
    return jnp.clip(values, min=-most, max=most).astype(held_as)


def setup_inputs(seed: int = 0) -> dict:
    arg_keys = jax.random.split(jax.random.key(seed), 21)
    inputs = centred(arg_keys[0], (SEQS, SEQ_LEN, D), 1.0, 6.0, ((0, 8), (1, 4)))
    cotangent = centred(arg_keys[1], (SEQS, SEQ_LEN, D), 1.0, 6.0, ((0, 8), (1, 4)))
    max_exit = draw_max_exit(jax.random.fold_in(arg_keys[20], 71), 0)
    min_exit = draw_min_exit(jax.random.fold_in(arg_keys[20], 71), 0)
    layer = draw_layer(jax.random.fold_in(arg_keys[20], 71), 0)
    wq = centred(arg_keys[5], (D, D), D ** -0.5, 0.125, ((0, 32),))
    wk = centred(arg_keys[6], (D, D), D ** -0.5, 0.125, ((0, 32),))
    wv = centred(arg_keys[7], (D, D), D ** -0.5, 0.125, ((0, 32),))
    wo = centred(arg_keys[8], (D, D), (D // 16) ** -0.5, 0.5, ((0, 32),))
    gain_one = jnp.clip(1.0 + 0.15 * jax.random.normal(arg_keys[9], (D,), jnp.float32), 0.25, 1.75).astype(jnp.bfloat16)
    shift_one = centred(arg_keys[10], (D,), 0.3, 3.0, ((0, 32),))
    bias_q = centred(arg_keys[11], (D,), 0.3, 3.0, ((0, 32),))
    bias_v = centred(arg_keys[12], (D,), 0.3, 3.0, ((0, 32),))
    bias_o = centred(arg_keys[13], (D,), 0.3, 3.0, ((0, 32),))
    w_in = centred(arg_keys[14], (D, FF), D ** -0.5, 0.125, ((0, 32),))
    w_out = centred(arg_keys[15], (FF, D), (FF // 2) ** -0.5, 0.09375, ((0, 32),))
    gain_two = jnp.clip(1.0 + 0.15 * jax.random.normal(arg_keys[16], (D,), jnp.float32), 0.25, 1.75).astype(jnp.bfloat16)
    shift_two = centred(arg_keys[17], (D,), 0.3, 3.0, ((0, 32),))
    bias_in = centred(arg_keys[18], (FF,), 0.5, 3.0, ((0, 32),))
    bias_out = centred(arg_keys[19], (D,), 0.3, 3.0, ((0, 32),))
    return dict(inputs=inputs, cotangent=cotangent, max_exit=max_exit, min_exit=min_exit, layer=layer, wq=wq, wk=wk, wv=wv, wo=wo, gain_one=gain_one, shift_one=shift_one, bias_q=bias_q, bias_v=bias_v, bias_o=bias_o, w_in=w_in, w_out=w_out, gain_two=gain_two, shift_two=shift_two, bias_in=bias_in, bias_out=bias_out)


epsilon = 1e-05
highest = lax.Precision.HIGHEST

@jax.custom_vjp
def low(v):
    return lax.optimization_barrier(v.astype(jnp.bfloat16)).astype(jnp.float32)

@jax.custom_vjp
def low_back(v):
    return v

def low_keep(v):
    return (low(v), None)

def low_pass(kept, grad):
    return (grad,)

def back_keep(v):
    return (v, None)

def back_low(kept, grad):
    return (low(grad),)
low.defvjp(low_keep, low_pass)
low_back.defvjp(back_keep, back_low)

def layer_norm(values_in, norm_gain, norm_shift):
    average = lax.optimization_barrier(jnp.mean(values_in, -1, keepdims=True))
    centered = values_in - average
    spread = lax.optimization_barrier(jnp.mean(centered * centered, -1, keepdims=True))
    return centered * lax.rsqrt(spread + epsilon) * norm_gain + norm_shift

def active_rows(max_exit, min_exit, layer):
    places = jnp.arange(SEQ_LEN, dtype=jnp.int32)
    exits = max_exit[:, None] - (max_exit - min_exit)[:, None] * places[None, :] // (SEQ_LEN - 1)
    return (layer[0] < exits).astype(jnp.float32)

def one_head(members):
    query, keys, values = members
    places = jnp.arange(SEQ_LEN, dtype=jnp.int32)
    causal = places[:, None] >= places[None, :]
    raw = low_back(jnp.dot(query, keys.T, precision=highest))
    logits = jnp.where(causal, raw * HEAD_DIM ** (-0.5), -1e+30)
    top = lax.optimization_barrier(jnp.max(logits, -1, keepdims=True))
    weights = jnp.exp(logits - top)
    probs = weights / lax.optimization_barrier(jnp.sum(weights, -1, keepdims=True))
    return jnp.dot(low(probs), values, precision=highest)

def heads_first(tensor):
    return tensor.reshape(SEQ_LEN, HEADS, HEAD_DIM).transpose(1, 0, 2)

def forward(params, inputs, active):
    wq, wk, wv, wo, gain_one, shift_one, bias_q, bias_v, bias_o, w_in, w_out, gain_two, shift_two, bias_in, bias_out = params
    normalized_rows = low(layer_norm(inputs, gain_one, shift_one))
    query = low(low_back(jnp.dot(normalized_rows, wq, precision=highest) + bias_q))
    keys = low(low_back(jnp.dot(normalized_rows, wk, precision=highest)))
    values = low(low_back(jnp.dot(normalized_rows, wv, precision=highest) + bias_v))
    mixed = lax.map(jax.checkpoint(one_head), (heads_first(query), heads_first(keys), heads_first(values)))
    attended_context = low(low_back(mixed.transpose(1, 0, 2).reshape(SEQ_LEN, D)))
    branch = low_back(jnp.dot(attended_context, wo, precision=highest) + bias_o)
    middle = inputs + active[:, None] * branch
    second_normalized_rows = low(layer_norm(middle, gain_two, shift_two))
    hidden_pre = low_back(jnp.dot(second_normalized_rows, w_in, precision=highest) + bias_in)
    hidden_state = low(jax.nn.gelu(hidden_pre, approximate=False))
    branch_two = low_back(jnp.dot(hidden_state, w_out, precision=highest) + bias_out)
    return middle + active[:, None] * branch_two

def reference(inputs, cotangent, max_exit, min_exit, layer, wq, wk, wv, wo, gain_one, shift_one, bias_q, bias_v, bias_o, w_in, w_out, gain_two, shift_two, bias_in, bias_out):
    params = tuple((weight.astype(jnp.float32) for weight in (wq, wk, wv, wo, gain_one, shift_one, bias_q, bias_v, bias_o, w_in, w_out, gain_two, shift_two, bias_in, bias_out)))
    active = active_rows(max_exit, min_exit, layer)

    def advance(totals, members):
        seq_in, seq_cot, seq_active = members
        result, pullback = jax.vjp(lambda weights_all, values_in: forward(weights_all, values_in, seq_active), params, seq_in.astype(jnp.float32))
        grads, grad_in = pullback(seq_cot.astype(jnp.float32))
        totals = jax.tree.map(lambda first, second: first + second, totals, grads)
        return (totals, (result.astype(jnp.bfloat16), grad_in.astype(jnp.bfloat16)))
    initial = jax.tree.map(jnp.zeros_like, params)
    totals, (output, input_grad) = lax.scan(advance, initial, (inputs, cotangent, active))
    return (output, input_grad, totals[0], totals[1], totals[2], totals[3], totals[4], totals[5], totals[6], totals[7], totals[8], totals[9], totals[10], totals[11], totals[12], totals[13], totals[14])
```

```python
from functools import partial

import jax
import jax.numpy as jnp
import numpy as np
from jax import lax
from jax.experimental import pallas as pl
from jax.experimental.pallas import tpu as pltpu
from jax.sharding import PartitionSpec as P

HEAD_DIM = 64
PAIR = 2 * HEAD_DIM
epsilon = 1e-05
LOG2E = 1.4426950408889634
bf16, f32 = jnp.bfloat16, jnp.float32
ALL = ("batch", "seq")
VMEM_LIMIT = 56 * 1024 * 1024


def dot_nn(a, b):
    return jnp.dot(a, b, preferred_element_type=f32)


def dot_nt(a, b):
    return lax.dot_general(a, b, (((1,), (1,)), ((), ())), preferred_element_type=f32)


def dot_tn(a, b):
    return lax.dot_general(a, b, (((0,), (0,)), ((), ())), preferred_element_type=f32)


class Ring:
    def __init__(self, size):
        self.size = size
        self.order = [i ^ (i >> 1) for i in range(size)]
        self.place = [self.order.index(i) for i in range(size)]
        self.up = [(self.order[i], self.order[(i + 1) % size]) for i in range(size)]
        self.down = [(self.order[i], self.order[i - 1]) for i in range(size)]

    def mine(self):
        return jnp.array(self.place, jnp.int32)[lax.axis_index("seq")]

    def steps_to(self):
        return lax.rem(jnp.array(self.place, jnp.int32) - self.mine() + self.size, self.size)

    def gather(self, block):
        n, half = self.size, block.shape[0] // 2
        out = [None] * n
        out[0] = rising = falling = block
        for k in range(1, n // 2):
            rising = lax.ppermute(rising, "seq", self.up)
            falling = lax.ppermute(falling, "seq", self.down)
            out[n - k], out[k] = rising, falling
        first = lax.ppermute(rising[:half], "seq", self.up)
        last = lax.ppermute(falling[half:], "seq", self.down)
        out[n // 2] = jnp.concatenate([first, last])
        return jnp.concatenate(out)

    def scatter(self, total):
        n = self.size
        rows = total.shape[0] // n
        half = rows // 2
        part = [total[k * rows : (k + 1) * rows] for k in range(n)]
        rising = lax.ppermute(part[n // 2][:half], "seq", self.up)
        falling = lax.ppermute(part[n // 2][half:], "seq", self.down)
        if n == 2:
            return part[0].astype(f32) + jnp.concatenate([rising, falling]).astype(f32)
        for k in range(n // 2 - 1, 0, -1):
            up, down = part[k], part[n - k]
            if k == n // 2 - 1:
                up = jnp.concatenate([add16(up[:half], rising), up[half:]])
                down = jnp.concatenate([down[:half], add16(down[half:], falling)])
            else:
                up, down = add16(up, rising), add16(down, falling)
            rising = lax.ppermute(up, "seq", self.up)
            falling = lax.ppermute(down, "seq", self.down)
        return part[0].astype(f32) + rising.astype(f32) + falling.astype(f32)


def add16(a, b):
    return (a.astype(f32) + b.astype(f32)).astype(bf16)


def gather_small(block, devices):
    place = lax.axis_index(ALL)
    have, bit = block[None], 1
    while bit < devices:
        other = lax.ppermute(have, ALL, [(i, i ^ bit) for i in range(devices)])
        low = (place & bit) == 0
        have = jnp.concatenate([jnp.where(low, have, other), jnp.where(low, other, have)])
        bit *= 2
    return have


def scatter_small(total, devices):
    place = lax.axis_index(ALL)
    bit = devices // 2
    while bit >= 1:
        low = (place & bit) == 0
        keep = jnp.where(low, total[:bit], total[bit:])
        send = jnp.where(low, total[bit:], total[:bit])
        total = keep + lax.ppermute(send, ALL, [(i, i ^ bit) for i in range(devices)])
        bit //= 2
    return total[0]


def attend_kernel(blocks, rows, steps, q_ref, k_ref, v_ref, o_ref, lse_ref, keys, values_t):
    for a in range(blocks):
        here = pl.ds(pl.multiple_of(steps[a] * rows, rows), rows)
        keys[a * rows : (a + 1) * rows, :] = k_ref[here, :]
        values_t[:, a * rows : (a + 1) * rows] = v_ref[here, :].astype(f32).T.astype(bf16)
    lane = lax.broadcasted_iota(jnp.int32, (1, PAIR), 1)
    causal = lax.broadcasted_iota(jnp.int32, (rows, rows), 0) <= lax.broadcasted_iota(
        jnp.int32, (rows, rows), 1
    )
    scale = HEAD_DIM ** (-0.5) * LOG2E
    for i in range(blocks):
        here = pl.ds(pl.multiple_of(steps[i] * rows, rows), rows)
        query = q_ref[here, :]
        ahead = i * rows
        parts = []
        for head in range(2):
            own = (lane // HEAD_DIM == head).astype(bf16)
            lines = slice(head * HEAD_DIM, (head + 1) * HEAD_DIM)
            q_head = query * own
            diag = dot_nt(keys[ahead : ahead + rows, :], q_head) * scale
            diag = jnp.where(causal, diag, -1e30)
            top = jnp.max(diag, 0, keepdims=True)
            if i > 0:
                full = dot_nt(keys[:ahead, :], q_head) * scale
                top = jnp.maximum(top, jnp.max(full, 0, keepdims=True))
            diag = jnp.exp2(diag - top)
            total = jnp.sum(diag, 0, keepdims=True)
            mixed = dot_nn(values_t[lines, ahead : ahead + rows], diag.astype(bf16))
            if i > 0:
                full = jnp.exp2(full - top)
                total = total + jnp.sum(full, 0, keepdims=True)
                mixed = mixed + dot_nn(values_t[lines, :ahead], full.astype(bf16))
            parts.append(mixed / total)
            lse_ref[0, head : head + 1, ahead : ahead + rows] = top + jnp.log2(total)
        o_ref[here, :] = jnp.concatenate(parts).T.astype(bf16)


def attend(qkv, steps, blocks):
    tokens, width = qkv.shape[0], qkv.shape[1] // 3
    pairs, rows = width // PAIR, tokens // blocks
    column = lambda c: pl.BlockSpec((tokens, PAIR), lambda h, steps: (0, c * pairs + h))
    return pl.pallas_call(
        partial(attend_kernel, blocks, rows),
        out_shape=(
            jax.ShapeDtypeStruct((tokens, width), bf16),
            jax.ShapeDtypeStruct((pairs, 2, tokens), f32),
        ),
        grid_spec=pltpu.PrefetchScalarGridSpec(
            num_scalar_prefetch=1,
            grid=(pairs,),
            in_specs=[column(0), column(1), column(2)],
            out_specs=(column(0), pl.BlockSpec((1, 2, tokens), lambda h, steps: (h, 0, 0))),
            scratch_shapes=[pltpu.VMEM((tokens, PAIR), bf16), pltpu.VMEM((PAIR, tokens), bf16)],
        ),
        compiler_params=pltpu.CompilerParams(vmem_limit_bytes=VMEM_LIMIT),
        cost_estimate=pl.CostEstimate(
            flops=4 * tokens * tokens * width, bytes_accessed=8 * tokens * width,
            transcendentals=tokens * tokens * pairs,
        ),
        name="attend",
    )(steps, qkv, qkv, qkv)


def attend_back_kernel(
    blocks, rows, steps, q_ref, k_ref, v_ref, g_ref, lse_ref, d_ref, keys, keys_t, values, dk, dv, dk16, dv16
):
    @pl.when(pl.program_id(1) == 0)
    def _():
        for a in range(blocks):
            here = pl.ds(pl.multiple_of(steps[a] * rows, rows), rows)
            place = slice(a * rows, (a + 1) * rows)
            keys[place, :] = k_ref[here, :]
            keys_t[:, place] = k_ref[here, :].astype(f32).T.astype(bf16)
            values[place, :] = v_ref[here, :]
        dk[...] = jnp.zeros_like(dk)
        dv[...] = jnp.zeros_like(dv)
        lane = lax.broadcasted_iota(jnp.int32, (1, PAIR), 1)
        scaling = HEAD_DIM ** (-0.5)
        for i in range(blocks):
            here = pl.ds(pl.multiple_of(steps[i] * rows, rows), rows)
            query, grad = q_ref[here, :], g_ref[here, :]
            length = (i + 1) * rows
            causal = lax.broadcasted_iota(jnp.int32, (length, rows), 0) <= (
                lax.broadcasted_iota(jnp.int32, (length, rows), 1) + i * rows
            )
            parts = []
            for head in range(2):
                own = (lane // HEAD_DIM == head).astype(bf16)
                lines = slice(head * HEAD_DIM, (head + 1) * HEAD_DIM)
                q_head, g_head = query * own, grad * own
                lse = lse_ref[0, head : head + 1, i * rows : (i + 1) * rows]
                logits = dot_nt(keys[:length, :], q_head) * (scaling * LOG2E)
                probs = jnp.where(causal, jnp.exp2(logits - lse), 0.0)
                grad_probs = dot_nt(values[:length, :], g_head)
                inner = jnp.sum(grad_probs * probs, 0, keepdims=True)
                grad_raw = (probs * (grad_probs - inner) * scaling).astype(bf16)
                parts.append(dot_nn(keys_t[lines, :length], grad_raw))
                dk[:length, :] += dot_nn(grad_raw, q_head)
                dv[:length, :] += dot_nn(probs.astype(bf16), g_head)
            d_ref[here, :] = jnp.concatenate(parts).T.astype(bf16)
        for a in range(blocks):
            here = pl.ds(pl.multiple_of(steps[a] * rows, rows), rows)
            dk16[here, :] = dk[a * rows : (a + 1) * rows, :].astype(bf16)
            dv16[here, :] = dv[a * rows : (a + 1) * rows, :].astype(bf16)

    @pl.when(pl.program_id(1) == 1)
    def _():
        d_ref[...] = dk16[...]

    @pl.when(pl.program_id(1) == 2)
    def _():
        d_ref[...] = dv16[...]


def attend_back(qkv, grad_context, lse, steps, blocks):
    tokens, width = grad_context.shape
    pairs, rows = width // PAIR, tokens // blocks
    column = lambda c: pl.BlockSpec((tokens, PAIR), lambda h, c_out, steps: (0, c * pairs + h))
    wide = lambda dtype: pltpu.VMEM((tokens, PAIR), dtype)
    return pl.pallas_call(
        partial(attend_back_kernel, blocks, rows),
        out_shape=jax.ShapeDtypeStruct((tokens, 3 * width), bf16),
        grid_spec=pltpu.PrefetchScalarGridSpec(
            num_scalar_prefetch=1,
            grid=(pairs, 3),
            in_specs=[
                column(0), column(1), column(2), column(0),
                pl.BlockSpec((1, 2, tokens), lambda h, c_out, steps: (h, 0, 0)),
            ],
            out_specs=pl.BlockSpec((tokens, PAIR), lambda h, c_out, steps: (0, c_out * pairs + h)),
            scratch_shapes=[
                wide(bf16), pltpu.VMEM((PAIR, tokens), bf16), wide(bf16),
                wide(f32), wide(f32), wide(bf16), wide(bf16),
            ],
        ),
        compiler_params=pltpu.CompilerParams(vmem_limit_bytes=VMEM_LIMIT),
        cost_estimate=pl.CostEstimate(
            flops=10 * tokens * tokens * width, bytes_accessed=14 * tokens * width,
            transcendentals=tokens * tokens * pairs,
        ),
        name="attend_back",
    )(steps, qkv, qkv, qkv, grad_context, lse)


def norm_parts(rows):
    centered = rows - jnp.mean(rows, -1, keepdims=True)
    spread = jnp.mean(centered * centered, -1, keepdims=True)
    inverse = lax.rsqrt(spread + epsilon)
    return centered * inverse, inverse


def norm_back(grad, gain, unit, inverse):
    scaled = grad * gain
    return inverse * (
        scaled - jnp.mean(scaled, -1, keepdims=True) - unit * jnp.mean(scaled * unit, -1, keepdims=True)
    )


def gelu_both(pre):
    below = 0.5 * (1.0 + lax.erf(pre * (0.5**0.5)))
    density = jnp.exp(-0.5 * pre * pre) * ((2.0 * np.pi) ** -0.5)
    return pre * below, below + pre * density


def body(
    inputs, cotangent, max_exit, min_exit, layer, wq, wk, wv, wo, gain_one, shift_one, bias_q, bias_v,
    bias_o, w_in, w_out, gain_two, shift_two, bias_in, bias_out,
):
    B, S = lax.axis_size("batch"), lax.axis_size("seq")
    devices = B * S
    s = lax.axis_index("seq")
    slots, T, D = inputs.shape
    r, rw = wq.shape[0], w_out.shape[0]
    Dl, Fl = D // S, rw * B
    whole_heads = r % HEAD_DIM == 0
    ring = Ring(S)
    steps = ring.steps_to()

    places = s * T + jnp.arange(T, dtype=jnp.int32)
    exits = max_exit[:, None] - (max_exit - min_exit)[:, None] * places[None, :] // (S * T - 1)
    active = (layer[0] < exits).astype(f32)[..., None]

    small = (gain_one, shift_one, bias_q, bias_v, bias_o, gain_two, shift_two, bias_out)
    packed = gather_small(jnp.concatenate(small + (bias_in,)), devices)
    full = lambda k: packed[:, k * r : (k + 1) * r].reshape(D).astype(f32)
    mine = lambda k: (
        lax.dynamic_index_in_dim(packed.reshape(B, S, -1), s, 1, False)[:, k * r : (k + 1) * r]
        if whole_heads
        else lax.dynamic_slice(packed[:, k * r : (k + 1) * r].reshape(D), (s * Dl,), (Dl,))
    ).reshape(Dl).astype(f32)
    gain_a, shift_a, bias_o_full, gain_b, shift_b, bias_out_full = (full(k) for k in (0, 1, 4, 5, 6, 7))
    bias_qkv = jnp.concatenate([mine(2), jnp.zeros((Dl,), f32), mine(3)])
    bias_hidden = (
        lax.dynamic_index_in_dim(packed.reshape(B, S, -1), s, 1, False)[:, len(small) * r :]
        .reshape(Fl).astype(f32)
    )

    def heads_out(w):
        if whole_heads:
            return w.reshape(r, B, S, r).transpose(2, 0, 1, 3).reshape(S, r, Dl)
        return w.reshape(r, S, Dl).transpose(1, 0, 2)

    def heads_back(w):
        if whole_heads:
            return w.reshape(S, r, B, r).transpose(1, 2, 0, 3).reshape(r, D)
        return w.transpose(1, 0, 2).reshape(r, D)

    swap = lambda x: lax.all_to_all(x, "seq", split_axis=0, concat_axis=0, tiled=True)
    gather = lambda x: lax.all_gather(x, "batch", axis=0, tiled=True)
    scatter = lambda x: lax.psum_scatter(x, "batch", scatter_dimension=0, tiled=True)
    qkv_pieces = jnp.concatenate([heads_out(w) for w in (wq, wk, wv)], -1)
    w_qkv = gather(swap(qkv_pieces).reshape(S * r, 3 * Dl))
    if whole_heads:
        w_o = gather(wo)
    else:
        w_o = lax.dynamic_slice(lax.all_gather(wo, ALL, axis=0, tiled=True), (s * Dl, 0), (Dl, D))
    in_pieces = w_in.reshape(r, B, S, rw).transpose(2, 0, 1, 3).reshape(S, r, Fl)
    w_1 = gather(swap(in_pieces).reshape(S * r, Fl))
    w_2 = gather(w_out)

    start = inputs.astype(f32)
    grad_out = cotangent.astype(f32)
    grad_two = (active * grad_out).astype(bf16)

    normed, qkv, context, lse, middle, normed_two = [], [], [], [], [], []
    for i in range(slots):
        rows = ring.gather(inputs[i]).astype(f32)
        unit, _ = norm_parts(rows)
        normed.append((unit * gain_a + shift_a).astype(bf16))
        qkv.append((dot_nn(normed[i], w_qkv) + bias_qkv).astype(bf16))
        mixed, log_total = attend(qkv[i], steps, S)
        context.append(mixed)
        lse.append(log_total)
        branch = ring.scatter(dot_nn(mixed, w_o).astype(bf16)) + bias_o_full
        middle.append(start[i] + active[i] * branch)
    unit_two, inverse_two = [], []
    for i in range(slots):
        unit, inverse = norm_parts(middle[i])
        unit_two.append(unit)
        inverse_two.append(inverse)
        normed_two.append(ring.gather((unit * gain_b + shift_b).astype(bf16)))
    grad_branch_two = [ring.gather(grad_two[i]) for i in range(slots)]

    hidden, grad_pre, output, grad_middle, grad_branch = [], [], [], [], []
    sum_gain_two = sum_shift_two = 0.0
    own_grad_branch = []
    for i in range(slots):
        value, slope = gelu_both(dot_nn(normed_two[i], w_1) + bias_hidden)
        hidden.append(value.astype(bf16))
        grad_pre.append((dot_nt(grad_branch_two[i], w_2) * slope).astype(bf16))
        back = ring.scatter(dot_nt(grad_pre[i], w_1).astype(bf16))
        sum_gain_two += jnp.sum(back * unit_two[i], 0)
        sum_shift_two += jnp.sum(back, 0)
        grad_middle.append(grad_out[i] + norm_back(back, gain_b, unit_two[i], inverse_two[i]))
        own_grad_branch.append((active[i] * grad_middle[i]).astype(bf16))
        grad_branch.append(ring.gather(own_grad_branch[i]))
        branch_two = ring.scatter(dot_nn(hidden[i], w_2).astype(bf16)) + bias_out_full
        output.append((middle[i] + active[i] * branch_two).astype(bf16))

    both = lambda left, right: sum(dot_tn(a, b) for a, b in zip(left, right))
    sum_w_1 = scatter(both(normed_two, grad_pre).astype(bf16))
    sum_w_1 = swap(sum_w_1.reshape(S, r, Fl)).reshape(S, r, B, rw).transpose(1, 2, 0, 3).reshape(r, -1)
    sum_w_2 = scatter(both(hidden, grad_branch_two).astype(bf16))

    grad_qkv, input_grad = [], []
    sum_gain_one = sum_shift_one = 0.0
    for i in range(slots):
        grad_context = dot_nt(grad_branch[i], w_o).astype(bf16)
        grad_qkv.append(attend_back(qkv[i], grad_context, lse[i], steps, S))
        back = ring.scatter(dot_nt(grad_qkv[i], w_qkv).astype(bf16))
        unit, inverse = norm_parts(start[i])
        sum_gain_one += jnp.sum(back * unit, 0)
        sum_shift_one += jnp.sum(back, 0)
        input_grad.append((grad_middle[i] + norm_back(back, gain_a, unit, inverse)).astype(bf16))

    sum_o = both(context, grad_branch)
    if whole_heads:
        sum_o = scatter(sum_o.astype(bf16))
    else:
        sum_o = lax.dynamic_update_slice(jnp.zeros((D, D), f32), sum_o, (s * Dl, 0))
        sum_o = lax.psum_scatter(sum_o.astype(bf16), ALL, scatter_dimension=0, tiled=True)
    sum_qkv = scatter(both(normed, grad_qkv).astype(bf16))
    sum_qkv = swap(sum_qkv.reshape(S, r, 3 * Dl))
    sum_q, sum_k, sum_v = (heads_back(sum_qkv[:, :, c * Dl : (c + 1) * Dl]) for c in range(3))

    tokens = lambda parts: sum(jnp.sum(p.astype(f32), 0) for p in parts)
    bias_sums = tokens(grad_qkv)
    plain = lambda v: v.reshape(devices, r)

    def own_heads(v):
        if whole_heads:
            spread = jnp.zeros((B, S, r), f32)
            return lax.dynamic_update_slice(spread, v.reshape(B, 1, r), (0, s, 0)).reshape(devices, r)
        return lax.dynamic_update_slice(jnp.zeros((D,), f32), v, (s * Dl,)).reshape(devices, r)

    own_hidden = lax.dynamic_update_slice(
        jnp.zeros((B, S, rw), f32), tokens(grad_pre).reshape(B, 1, rw), (0, s, 0)
    ).reshape(devices, rw)
    sums = scatter_small(
        jnp.concatenate(
            [
                plain(sum_gain_one), plain(sum_shift_one), own_heads(bias_sums[:Dl]),
                own_heads(bias_sums[2 * Dl :]), plain(tokens(own_grad_branch)), plain(sum_gain_two),
                plain(sum_shift_two), plain(tokens([grad_two[i] for i in range(slots)])), own_hidden,
            ],
            -1,
        ),
        devices,
    )
    g1, s1, bq, bv, bo, g2, s2, b2 = (sums[k * r : (k + 1) * r] for k in range(8))
    wide = lambda v: v.astype(f32)
    return (
        jnp.stack(output), jnp.stack(input_grad), wide(sum_q), wide(sum_k), wide(sum_v), wide(sum_o),
        g1, s1, bq, bv, bo, wide(sum_w_1), wide(sum_w_2), g2, s2, sums[8 * r :], b2,
    )


def solution(mesh):
    tokens, rows, vector = P("batch", "seq", None), P(ALL, None), P(ALL)
    placed = (
        (tokens, tokens, P("batch"), P("batch"), P())
        + (rows,) * 4 + (vector,) * 5 + (rows,) * 2 + (vector,) * 4
    )
    out = (tokens, tokens) + (rows,) * 4 + (vector,) * 5 + (rows,) * 2 + (vector,) * 4
    return jax.shard_map(body, mesh=mesh, in_specs=placed, out_specs=out, check_vma=False)
```

```python
from functools import partial

import jax
import jax.numpy as jnp
import numpy as np
from jax import lax
from jax.experimental import pallas as pl
from jax.experimental.pallas import tpu as pltpu
from jax.sharding import PartitionSpec as P

HEAD_DIM = 64
PAIR = 2 * HEAD_DIM
epsilon = 1e-05
LOG2E = 1.4426950408889634
bf16, f32 = jnp.bfloat16, jnp.float32
ALL = ("batch", "seq")
VMEM_LIMIT = 56 * 1024 * 1024


def dot_nn(a, b):
    return jnp.dot(a, b, preferred_element_type=f32)


def dot_nt(a, b):
    return lax.dot_general(a, b, (((1,), (1,)), ((), ())), preferred_element_type=f32)


def dot_tn(a, b):
    return lax.dot_general(a, b, (((0,), (0,)), ((), ())), preferred_element_type=f32)


PARAMS = pltpu.CompilerParams(vmem_limit_bytes=VMEM_LIMIT)
PACE = 0.5


def cost(flops):
    return pl.CostEstimate(flops=int(PACE * flops), bytes_accessed=int(PACE * flops / 320), transcendentals=0)


def tile_of(width, most=512):
    return next(t for t in (most, 256, 128, width) if width % t == 0)


def listed(value):
    return list(value) if isinstance(value, (list, tuple)) else [value]


def rows_of(pieces):
    return sum(p.shape[0] for p in pieces)


def fixed(shape):
    return pl.BlockSpec(shape, lambda j: (0,) * len(shape))


def join(refs, whole):
    at = 0
    for ref in refs:
        whole[at : at + ref.shape[0], :] = ref[...]
        at += ref.shape[0]


def first_step(body):
    pl.when(pl.program_id(0) == 0)(body)


def matmul(left, right, dot, parts=None):
    left = listed(left)
    n, rows, depth = len(left), rows_of(left), left[0].shape[1]
    width = right.shape[1] if dot is dot_nn else right.shape[0]
    tile, ranges = tile_of(width), parts or [[(0, rows)]]
    sizes = [sum(stop - begin for begin, stop in part) for part in ranges]

    def kernel(*refs):
        whole = refs[0]
        if n > 1:
            whole = refs[-1]
            first_step(lambda: join(refs[:n], whole))
        total = dot(whole[...], refs[n][...]).astype(bf16)
        for ref, part in zip(refs[n + 1 :], ranges):
            at = 0
            for begin, stop in part:
                ref[at : at + stop - begin, :] = total[begin:stop]
                at += stop - begin

    strip = (
        pl.BlockSpec((depth, tile), lambda j: (0, j)) if dot is dot_nn else pl.BlockSpec((tile, depth), lambda j: (j, 0))
    )
    out = pl.pallas_call(
        kernel,
        out_shape=tuple(jax.ShapeDtypeStruct((size, width), bf16) for size in sizes),
        grid=(width // tile,),
        in_specs=[fixed(p.shape) for p in left] + [strip],
        out_specs=tuple(pl.BlockSpec((size, tile), lambda j: (0, j)) for size in sizes),
        scratch_shapes=[pltpu.VMEM((rows, depth), bf16)] if n > 1 else [],
        compiler_params=PARAMS, cost_estimate=cost(3.5 * rows * depth * width), name="matmul",
    )(*left, right)
    return out if parts else out[0]


def weight_sum(lefts, rights):
    lefts, rights = [listed(v) for v in lefts], [listed(v) for v in rights]
    tokens = [rows_of(v) for v in lefts]
    rows, width = lefts[0][0].shape[1], rights[0][0].shape[1]
    tile = tile_of(rows, 256)
    sizes = [len(v) for v in lefts + rights]
    spots = [pltpu.VMEM((t, tile), bf16) for t in tokens] + [pltpu.VMEM((t, width), bf16) for t in tokens]
    spots = [spot if size > 1 else pltpu.VMEM((16, 128), bf16) for spot, size in zip(spots, sizes)]
    n = len(lefts)

    def kernel(*refs):
        out, spot, at, wholes = refs[sum(sizes)], refs[sum(sizes) + 1 :], 0, []
        for k, size in enumerate(sizes):
            group = refs[at : at + size]
            at += size
            if size == 1:
                wholes.append(group[0])
                continue
            wholes.append(spot[k])
            if k < n:
                join(group, spot[k])
            else:
                first_step(partial(join, group, spot[k]))
        total = sum(dot_tn(wholes[k][...], wholes[n + k][...]) for k in range(n))
        out[...] = total.astype(bf16)

    return pl.pallas_call(
        kernel,
        out_shape=jax.ShapeDtypeStruct((rows, width), bf16),
        grid=(rows // tile,),
        in_specs=[pl.BlockSpec((p.shape[0], tile), lambda j: (0, j)) for v in lefts for p in v]
        + [fixed(p.shape) for v in rights for p in v],
        out_specs=pl.BlockSpec((tile, width), lambda j: (j, 0)),
        scratch_shapes=spots,
        compiler_params=PARAMS, cost_estimate=cost(3.3 * sum(tokens) * rows * width), name="weight_sum",
    )(*(p for v in lefts + rights for p in v))


def norm_parts(rows):
    centered = rows - jnp.mean(rows, -1, keepdims=True)
    spread = jnp.mean(centered * centered, -1, keepdims=True)
    inverse = lax.rsqrt(spread + epsilon)
    return centered * inverse, inverse


def norm_back(grad, gain, unit, inverse):
    scaled = grad * gain
    return inverse * (
        scaled - jnp.mean(scaled, -1, keepdims=True) - unit * jnp.mean(scaled * unit, -1, keepdims=True)
    )


def project(pieces, gain, shift, w_qkv, bias):
    n, rows, (depth, width) = len(pieces), rows_of(pieces), w_qkv.shape
    tile = tile_of(width)

    def kernel(*refs):
        gain_ref, shift_ref, w_ref, bias_ref, normed, out = refs[n:]

        def norm():
            at = 0
            for ref in refs[:n]:
                for k in range(0, ref.shape[0], 64):
                    unit, _ = norm_parts(ref[k : k + 64, :].astype(f32))
                    normed[at + k : at + k + 64, :] = (unit * gain_ref[...] + shift_ref[...]).astype(bf16)
                at += ref.shape[0]

        first_step(norm)
        out[...] = (dot_nn(normed[...], w_ref[...]) + bias_ref[...]).astype(bf16)

    return pl.pallas_call(
        kernel,
        out_shape=(jax.ShapeDtypeStruct((rows, depth), bf16), jax.ShapeDtypeStruct((rows, width), bf16)),
        grid=(width // tile,),
        in_specs=[fixed(p.shape) for p in pieces]
        + [fixed((1, depth)), fixed((1, depth)), pl.BlockSpec((depth, tile), lambda j: (0, j)), pl.BlockSpec((1, tile), lambda j: (0, j))],
        out_specs=(fixed((rows, depth)), pl.BlockSpec((rows, tile), lambda j: (0, j))),
        compiler_params=PARAMS, cost_estimate=cost(5 * rows * depth * width), name="project",
    )(*pieces, gain, shift, w_qkv, bias)


def gelu_both(pre):
    below = 0.5 * (1.0 + lax.erf(pre * (0.5**0.5)))
    density = jnp.exp(-0.5 * pre * pre) * ((2.0 * np.pi) ** -0.5)
    return pre * below, below + pre * density


def hidden_both(normed, grad_hidden, w_1, bias):
    n, rows, (depth, width) = len(normed), rows_of(normed), w_1.shape
    tile = tile_of(width)

    def kernel(*refs):
        g_ref, w1_ref, b_ref, h_ref, p_ref, s_ref, whole = refs[n:]
        first_step(lambda: join(refs[:n], whole))
        value, slope = gelu_both(dot_nn(whole[...], w1_ref[...]) + b_ref[...])
        h_ref[...] = value.astype(bf16)
        grad_pre = (g_ref[...].astype(f32) * slope).astype(bf16)
        p_ref[...] = grad_pre
        s_ref[...] = jnp.sum(grad_pre.astype(f32), 0, keepdims=True)

    part = pl.BlockSpec((rows, tile), lambda j: (0, j))
    line = pl.BlockSpec((1, tile), lambda j: (0, j))
    return pl.pallas_call(
        kernel,
        out_shape=(jax.ShapeDtypeStruct((rows, width), bf16),) * 2 + (jax.ShapeDtypeStruct((1, width), f32),),
        grid=(width // tile,),
        in_specs=[fixed(p.shape) for p in normed] + [part, pl.BlockSpec((depth, tile), lambda j: (0, j)), line],
        out_specs=(part, part, line),
        scratch_shapes=[pltpu.VMEM((rows, depth), bf16)],
        compiler_params=PARAMS, cost_estimate=cost(5 * rows * depth * width), name="hidden_both",
    )(*normed, grad_hidden, w_1, bias)


STEP = 64


def own_rows(depth):
    return pl.BlockSpec((STEP, depth), lambda j: (j, 0))


def slot_rows(slot, depth):
    return pl.BlockSpec((1, STEP, depth), lambda j: (slot, j, 0))


def summed_rows(rows, depth):
    half = rows // 2 // STEP
    spec = lambda place: pl.BlockSpec((STEP, depth), lambda j: (place(j), 0))
    return [
        own_rows(depth), spec(lambda j: jnp.maximum(j, half)), spec(lambda j: jnp.minimum(j, half - 1) + half),
        spec(lambda j: jnp.minimum(j, half - 1)), spec(lambda j: jnp.maximum(j - half, 0)),
    ]


def summed(refs, steps):
    own, up, down, far_up, far_down = (ref[...].astype(f32) for ref in refs)
    early = pl.program_id(0) < steps // 2
    return own + jnp.where(early, far_up, up) + jnp.where(early, down, far_down)


def second_norm(slot, branch, inputs, active, bias, gain, shift):
    rows, depth = branch[0].shape

    def kernel(*refs):
        x, act, bias_ref, gain_ref, shift_ref, middle, normed = refs[5:]
        total = summed(refs[:5], rows // STEP) + bias_ref[...]
        total = x[0].astype(f32) + act[...] * total
        middle[...] = total
        normed[...] = (norm_parts(total)[0] * gain_ref[...] + shift_ref[...]).astype(bf16)

    return pl.pallas_call(
        kernel,
        out_shape=(jax.ShapeDtypeStruct((rows, depth), f32), jax.ShapeDtypeStruct((rows, depth), bf16)),
        grid=(rows // STEP,),
        in_specs=summed_rows(rows, depth) + [slot_rows(slot, depth), own_rows(1)] + [fixed((1, depth))] * 3,
        out_specs=(own_rows(depth), own_rows(depth)),
        compiler_params=PARAMS, cost_estimate=cost(6e9), name="second_norm",
    )(*branch, inputs, active, bias, gain, shift)


def add_line(sums, line, value):
    sums[line : line + 1, :] += jnp.sum(value, 0, keepdims=True)


def second_norm_back(slot, back, middle, cotangent, active, gain):
    rows, depth = middle.shape

    def kernel(*refs):
        mid, cot, act, gain_ref, grad_middle, grad_branch, sums = refs[5:]

        @first_step
        def _():
            sums[...] = jnp.zeros_like(sums)

        grad = summed(refs[:5], rows // STEP)
        unit, inverse = norm_parts(mid[...])
        outer = cot[0].astype(f32)
        total = outer + norm_back(grad, gain_ref[...], unit, inverse)
        grad_middle[...] = total
        branch = (act[...] * total).astype(bf16)
        grad_branch[...] = branch
        add_line(sums, 0, grad * unit)
        add_line(sums, 1, grad)
        add_line(sums, 2, branch.astype(f32))
        add_line(sums, 3, (act[...] * outer).astype(bf16).astype(f32))

    return pl.pallas_call(
        kernel,
        out_shape=(
            jax.ShapeDtypeStruct((rows, depth), f32), jax.ShapeDtypeStruct((rows, depth), bf16),
            jax.ShapeDtypeStruct((8, depth), f32),
        ),
        grid=(rows // STEP,),
        in_specs=summed_rows(rows, depth) + [own_rows(depth), slot_rows(slot, depth), own_rows(1), fixed((1, depth))],
        out_specs=(own_rows(depth), own_rows(depth), fixed((8, depth))),
        compiler_params=PARAMS, cost_estimate=cost(7e9), name="second_norm_back",
    )(*back, middle, cotangent, active, gain)


def first_norm_back(slot, back, inputs, grad_middle, gain, others):
    (rows, depth), slots = grad_middle.shape, inputs.shape[0]
    more = [] if others is None else [others]

    def kernel(*refs):
        x, grad_mid, gain_ref = refs[5:8]
        out, sums = refs[-2:]

        @first_step
        def _():
            sums[...] = jnp.zeros_like(sums)

        grad = summed(refs[:5], rows // STEP)
        unit, inverse = norm_parts(x[0].astype(f32))
        out[0] = (grad_mid[...] + norm_back(grad, gain_ref[...], unit, inverse)).astype(bf16)
        add_line(sums, 0, grad * unit)
        add_line(sums, 1, grad)

    return pl.pallas_call(
        kernel,
        out_shape=(jax.ShapeDtypeStruct((slots, rows, depth), bf16), jax.ShapeDtypeStruct((8, depth), f32)),
        grid=(rows // STEP,),
        in_specs=summed_rows(rows, depth) + [slot_rows(slot, depth), own_rows(depth), fixed((1, depth))]
        + [pl.BlockSpec(memory_space=pl.ANY)] * len(more),
        out_specs=(slot_rows(slot, depth), fixed((8, depth))),
        input_output_aliases={8: 0} if more else {},
        compiler_params=PARAMS, cost_estimate=cost(7e9), name="first_norm_back",
    )(*back, inputs, grad_middle, gain, *more)


def final_sum(slot, slots, branch, middle, active, bias, others):
    rows, depth = middle.shape
    more = [] if others is None else [others]

    def kernel(*refs):
        mid, act, bias_ref = refs[5:8]
        total = summed(refs[:5], rows // STEP) + bias_ref[...]
        refs[-1][0] = (mid[...] + act[...] * total).astype(bf16)

    return pl.pallas_call(
        kernel,
        out_shape=jax.ShapeDtypeStruct((slots, rows, depth), bf16),
        grid=(rows // STEP,),
        in_specs=summed_rows(rows, depth) + [own_rows(depth), own_rows(1), fixed((1, depth))] + [pl.BlockSpec(memory_space=pl.ANY)] * len(more),
        out_specs=slot_rows(slot, depth),
        input_output_aliases={8: 0} if more else {},
        compiler_params=PARAMS, cost_estimate=cost(6e9), name="final_sum",
    )(*branch, middle, active, bias, *more)


def head_pieces(weights, groups, blocks):
    rows = weights[0].shape[0]

    def kernel(*refs):
        for k in range(blocks):
            strips = [ref[:, (g * blocks + k) * rows : (g * blocks + k + 1) * rows] for ref in refs[:-1] for g in range(groups)]
            refs[-1][k] = jnp.concatenate(strips, 1)

    return pl.pallas_call(
        kernel,
        out_shape=jax.ShapeDtypeStruct((blocks, rows, 3 * groups * rows), bf16),
        compiler_params=PARAMS, cost_estimate=cost(2e9), name="head_pieces",
    )(*weights)


def unit_pieces(weight, groups, blocks):
    (rows, width), n = weight.shape, weight.shape[1] // (groups * blocks)

    def kernel(ref, out):
        for k in range(blocks):
            for g in range(groups):
                out[k, :, g * n : (g + 1) * n] = ref[:, (g * blocks + k) * n : (g * blocks + k + 1) * n]

    return pl.pallas_call(
        kernel,
        out_shape=jax.ShapeDtypeStruct((blocks, rows, groups * n), bf16),
        compiler_params=PARAMS, cost_estimate=cost(2e9), name="unit_pieces",
    )(weight) if n % 128 == 0 else weight.reshape(rows, groups, blocks, n).transpose(2, 0, 1, 3).reshape(blocks, rows, groups * n)


def unit_rows(pieces, groups):
    blocks, rows, width = pieces.shape
    n = width // groups

    def kernel(ref, out):
        for k in range(blocks):
            for g in range(groups):
                out[:, (g * blocks + k) * n : (g * blocks + k + 1) * n] = ref[k, :, g * n : (g + 1) * n].astype(f32)

    return pl.pallas_call(
        kernel,
        out_shape=jax.ShapeDtypeStruct((rows, blocks * width), f32),
        compiler_params=PARAMS, cost_estimate=cost(2e9), name="unit_rows",
    )(pieces) if n % 128 == 0 else pieces.reshape(blocks, rows, groups, n).transpose(1, 2, 0, 3).reshape(rows, -1).astype(f32)


def head_rows(pieces, groups):
    blocks, rows, width = pieces.shape

    def kernel(ref, *outs):
        for c, out in enumerate(outs):
            strips = [
                ref[k, :, (c * groups + g) * rows : (c * groups + g + 1) * rows] for g in range(groups) for k in range(blocks)
            ]
            out[...] = jnp.concatenate(strips, 1).astype(f32)

    return pl.pallas_call(
        kernel,
        out_shape=(jax.ShapeDtypeStruct((rows, blocks * width // 3), f32),) * 3,
        compiler_params=PARAMS, cost_estimate=cost(2e9), name="head_rows",
    )(pieces)


def after(value, others):
    return value if others is None else lax.optimization_barrier((value, others))[0]


class Clock:
    def __init__(self):
        self.last = None

    def now(self, value):
        return after(value, self.last)

    def did(self, value):
        self.last = jax.tree.leaves(value)
        return value


class Ring:
    def __init__(self, size):
        self.size = size
        self.order = [i ^ (i >> 1) for i in range(size)]
        self.place = [self.order.index(i) for i in range(size)]

    def parts(self, rows):
        n, half = self.size, rows // 2
        first = lambda k: (k * rows, k * rows + half)
        second = lambda k: (k * rows + half, (k + 1) * rows)
        far = n // 2
        out = [[(0, rows)], [first(far), second(far - 1)], [second(far), first(far + 1)]]
        for k in range(far - 1, 1, -1):
            out += [[first(k)], [second(k - 1)], [second(n - k)], [first(n - k + 1)]]
        return out + [[first(1)], [second(n - 1)]]

    def send(self, value, steps):
        n = self.size
        return lax.ppermute(value, "seq", [(self.order[i], self.order[(i + steps) % n]) for i in range(n)])

    def mine(self):
        place, shift = lax.axis_index("seq"), 1
        while shift < self.size:
            place = place ^ (place >> shift)
            shift *= 2
        return place

    def at(self, steps):
        place = (self.mine() + steps) & (self.size - 1)
        return place ^ (place >> 1)

    def steps_to(self):
        return (jnp.array(self.place, jnp.int32) - self.mine()) & (self.size - 1)

    def swap(self, pieces):
        take = lambda k: lax.dynamic_slice_in_dim(pieces, self.at(k), 1)
        out = lax.dynamic_update_slice_in_dim(jnp.zeros_like(pieces), take(0), self.at(0), 0)
        for k in range(1, self.size):
            came = self.send(take(k), k)
            out = lax.dynamic_update_slice_in_dim(out, came, self.at(-k), 0)
        return out


class Gather:
    def __init__(self, ring, clock, block):
        self.ring, self.clock = ring, clock
        self.half = block.shape[0] // 2
        self.near, self.far = [block], []
        block = clock.now(block)
        self.rising, self.falling = ring.send(block, 1), ring.send(block, -1)

    def go(self):
        ring = self.ring
        for _ in range(2, ring.size // 2):
            self.far.append(self.rising)
            self.near.append(self.falling)
            self.rising, self.falling = ring.send(self.rising, 1), ring.send(self.falling, -1)
        rising, falling = self.clock.did(self.clock.now((self.rising, self.falling)))
        self.far.append(rising)
        self.near.append(falling)
        first, second = self.clock.did((rising[: self.half], falling[self.half :]))
        self.middle = [ring.send(first, 1), ring.send(second, -1)]

    def arrive(self):
        self.middle = list(self.clock.did(self.clock.now(tuple(self.middle))))

    def result(self):
        return self.clock.now(self.near + self.middle + self.far[::-1])


class Scatter:
    def __init__(self, ring, clock, part):
        self.ring, self.clock, self.part = ring, clock, part
        self.up, self.down = ring.send(part[1], 1), ring.send(part[2], -1)

    def go(self):
        n, send, now, did = self.ring.size, self.ring.send, self.clock.now, self.clock.did
        half = self.part[1].shape[0] // 2
        rest = self.part[3:]
        for k in range(0, 4 * (n // 2 - 2), 4):
            up = jnp.concatenate([add16(rest[k], self.up[:half]), add16(rest[k + 1], self.up[half:])])
            down = jnp.concatenate([add16(rest[k + 2], self.down[:half]), add16(rest[k + 3], self.down[half:])])
            self.up, self.down = send(up, 1), send(down, -1)
        up, down = did(now((self.up, self.down)))
        far_up, far_down = did((add16(rest[-2], up[:half]), add16(rest[-1], down[:half])))
        self.up, self.down = up, down
        self.far_up, self.far_down = send(far_up, 1), send(far_down, -1)

    def arrive(self):
        self.far_up, self.far_down = self.clock.did(self.clock.now((self.far_up, self.far_down)))

    def result(self):
        return (self.part[0], self.up, self.down) + self.clock.now((self.far_up, self.far_down))


def add16(a, b):
    return (a.astype(f32) + b.astype(f32)).astype(bf16)


def gather_small(block, devices):
    place = lax.axis_index(ALL)
    have, bit = block[None], 1
    while bit < devices:
        other = lax.ppermute(have, ALL, [(i, i ^ bit) for i in range(devices)])
        low = (place & bit) == 0
        have = jnp.concatenate([jnp.where(low, have, other), jnp.where(low, other, have)])
        bit *= 2
    return have


class SmallScatter:
    def __init__(self, clock, total):
        self.clock, self.keep, self.came, self.devices = clock, total, None, total.shape[0]

    def gathered(self):
        total = self.clock.now(self.keep)
        return total if self.came is None else self.clock.did(total + self.clock.now(self.came))

    def step(self):
        bit = self.keep.shape[0] // 2
        if bit == 0:
            return
        total = self.gathered()
        low = (lax.axis_index(ALL) & bit) == 0
        self.keep = jnp.where(low, total[:bit], total[bit:])
        send = jnp.where(low, total[bit:], total[:bit])
        self.came = lax.ppermute(send, ALL, [(i, i ^ bit) for i in range(self.devices)])

    def result(self):
        while self.keep.shape[0] > 1:
            self.step()
        return self.gathered()[0]


def attend_kernel(blocks, rows, steps, q_ref, k_ref, v_ref, o_ref, lse_ref, keys, values_t):
    for a in range(blocks):
        here = pl.ds(pl.multiple_of(steps[a] * rows, rows), rows)
        keys[a * rows : (a + 1) * rows, :] = k_ref[here, :]
        values_t[:, a * rows : (a + 1) * rows] = v_ref[here, :].astype(f32).T.astype(bf16)
    lane = lax.broadcasted_iota(jnp.int32, (1, PAIR), 1)
    causal = lax.broadcasted_iota(jnp.int32, (rows, rows), 0) <= lax.broadcasted_iota(
        jnp.int32, (rows, rows), 1
    )
    scale = HEAD_DIM ** (-0.5) * LOG2E
    for i in range(blocks):
        here = pl.ds(pl.multiple_of(steps[i] * rows, rows), rows)
        query = q_ref[here, :]
        ahead = i * rows
        parts = []
        for head in range(2):
            own = (lane // HEAD_DIM == head).astype(bf16)
            lines = slice(head * HEAD_DIM, (head + 1) * HEAD_DIM)
            q_head = query * own
            diag = dot_nt(keys[ahead : ahead + rows, :], q_head) * scale
            diag = jnp.where(causal, diag, -1e30)
            top = jnp.max(diag, 0, keepdims=True)
            if i > 0:
                full = dot_nt(keys[:ahead, :], q_head) * scale
                top = jnp.maximum(top, jnp.max(full, 0, keepdims=True))
            diag = jnp.exp2(diag - top)
            total = jnp.sum(diag, 0, keepdims=True)
            mixed = dot_nn(values_t[lines, ahead : ahead + rows], diag.astype(bf16))
            if i > 0:
                full = jnp.exp2(full - top)
                total = total + jnp.sum(full, 0, keepdims=True)
                mixed = mixed + dot_nn(values_t[lines, :ahead], full.astype(bf16))
            parts.append(mixed / total)
            lse_ref[0, head : head + 1, ahead : ahead + rows] = top + jnp.log2(total)
        o_ref[here, :] = jnp.concatenate(parts).T.astype(bf16)


def attend(qkv, steps, blocks):
    tokens, width = qkv.shape[0], qkv.shape[1] // 3
    pairs, rows = width // PAIR, tokens // blocks
    column = lambda c: pl.BlockSpec((tokens, PAIR), lambda h, steps: (0, c * pairs + h))
    return pl.pallas_call(
        partial(attend_kernel, blocks, rows),
        out_shape=(
            jax.ShapeDtypeStruct((tokens, width), bf16),
            jax.ShapeDtypeStruct((pairs, 2, tokens), f32),
        ),
        grid_spec=pltpu.PrefetchScalarGridSpec(
            num_scalar_prefetch=1,
            grid=(pairs,),
            in_specs=[column(0), column(1), column(2)],
            out_specs=(column(0), pl.BlockSpec((1, 2, tokens), lambda h, steps: (h, 0, 0))),
            scratch_shapes=[pltpu.VMEM((tokens, PAIR), bf16), pltpu.VMEM((PAIR, tokens), bf16)],
        ),
        compiler_params=pltpu.CompilerParams(vmem_limit_bytes=VMEM_LIMIT),
        cost_estimate=cost(32 * tokens * tokens * width),
        name="attend",
    )(steps, qkv, qkv, qkv)


def attend_back_kernel(
    blocks, rows, steps, q_ref, k_ref, v_ref, g_ref, lse_ref, d_ref, keys, keys_t, values, dk, dv, dk16, dv16
):
    @pl.when(pl.program_id(1) == 0)
    def _():
        for a in range(blocks):
            here = pl.ds(pl.multiple_of(steps[a] * rows, rows), rows)
            place = slice(a * rows, (a + 1) * rows)
            keys[place, :] = k_ref[here, :]
            keys_t[:, place] = k_ref[here, :].astype(f32).T.astype(bf16)
            values[place, :] = v_ref[here, :]
        dk[...] = jnp.zeros_like(dk)
        dv[...] = jnp.zeros_like(dv)
        lane = lax.broadcasted_iota(jnp.int32, (1, PAIR), 1)
        scaling = HEAD_DIM ** (-0.5)
        for i in range(blocks):
            here = pl.ds(pl.multiple_of(steps[i] * rows, rows), rows)
            query, grad = q_ref[here, :], g_ref[here, :]
            length = (i + 1) * rows
            causal = lax.broadcasted_iota(jnp.int32, (length, rows), 0) <= (
                lax.broadcasted_iota(jnp.int32, (length, rows), 1) + i * rows
            )
            parts = []
            for head in range(2):
                own = (lane // HEAD_DIM == head).astype(bf16)
                lines = slice(head * HEAD_DIM, (head + 1) * HEAD_DIM)
                q_head, g_head = query * own, grad * own
                lse = lse_ref[0, head : head + 1, i * rows : (i + 1) * rows]
                logits = dot_nt(keys[:length, :], q_head) * (scaling * LOG2E)
                probs = jnp.where(causal, jnp.exp2(logits - lse), 0.0)
                grad_probs = dot_nt(values[:length, :], g_head)
                inner = jnp.sum(grad_probs * probs, 0, keepdims=True)
                grad_raw = (probs * (grad_probs - inner) * scaling).astype(bf16)
                parts.append(dot_nn(keys_t[lines, :length], grad_raw))
                dk[:length, :] += dot_nn(grad_raw, q_head)
                dv[:length, :] += dot_nn(probs.astype(bf16), g_head)
            d_ref[here, :] = jnp.concatenate(parts).T.astype(bf16)
        for a in range(blocks):
            here = pl.ds(pl.multiple_of(steps[a] * rows, rows), rows)
            dk16[here, :] = dk[a * rows : (a + 1) * rows, :].astype(bf16)
            dv16[here, :] = dv[a * rows : (a + 1) * rows, :].astype(bf16)

    @pl.when(pl.program_id(1) == 1)
    def _():
        d_ref[...] = dk16[...]

    @pl.when(pl.program_id(1) == 2)
    def _():
        d_ref[...] = dv16[...]


def attend_back(qkv, grad_context, lse, steps, blocks):
    tokens, width = grad_context.shape
    pairs, rows = width // PAIR, tokens // blocks
    column = lambda c: pl.BlockSpec((tokens, PAIR), lambda h, c_out, steps: (0, c * pairs + h))
    wide = lambda dtype: pltpu.VMEM((tokens, PAIR), dtype)
    return pl.pallas_call(
        partial(attend_back_kernel, blocks, rows),
        out_shape=jax.ShapeDtypeStruct((tokens, 3 * width), bf16),
        grid_spec=pltpu.PrefetchScalarGridSpec(
            num_scalar_prefetch=1,
            grid=(pairs, 3),
            in_specs=[
                column(0), column(1), column(2), column(0),
                pl.BlockSpec((1, 2, tokens), lambda h, c_out, steps: (h, 0, 0)),
            ],
            out_specs=pl.BlockSpec((tokens, PAIR), lambda h, c_out, steps: (0, c_out * pairs + h)),
            scratch_shapes=[
                wide(bf16), pltpu.VMEM((PAIR, tokens), bf16), wide(bf16),
                wide(f32), wide(f32), wide(bf16), wide(bf16),
            ],
        ),
        compiler_params=pltpu.CompilerParams(vmem_limit_bytes=VMEM_LIMIT),
        cost_estimate=cost(64 * tokens * tokens * width),
        name="attend_back",
    )(steps, qkv, qkv, qkv, grad_context, lse)


def body(
    inputs, cotangent, max_exit, min_exit, layer, wq, wk, wv, wo, gain_one, shift_one, bias_q, bias_v,
    bias_o, w_in, w_out, gain_two, shift_two, bias_in, bias_out,
):
    B, S = lax.axis_size("batch"), lax.axis_size("seq")
    devices = B * S
    s = lax.axis_index("seq")
    slots, T, D = inputs.shape
    r, rw = wq.shape[0], w_out.shape[0]
    Dl, Fl = D // S, rw * B
    whole_heads = r % HEAD_DIM == 0
    ring = Ring(S)
    steps = ring.steps_to()

    places = s * T + jnp.arange(T, dtype=jnp.int32)
    exits = max_exit[:, None] - (max_exit - min_exit)[:, None] * places[None, :] // (S * T - 1)
    active = (layer[0] < exits).astype(f32)[..., None]

    clock = Clock()
    grad_two = [(active[i] * cotangent[i].astype(f32)).astype(bf16) for i in range(slots)]
    gather = lambda x: lax.all_gather(x, "batch", axis=0, tiled=True)
    scatter = lambda x: lax.psum_scatter(x, "batch", scatter_dimension=0, tiled=True)
    qkv_pieces = (
        head_pieces((wq, wk, wv), B, S)
        if whole_heads
        else jnp.concatenate([w.reshape(r, S, Dl).transpose(1, 0, 2) for w in (wq, wk, wv)], -1)
    )
    in_pieces = unit_pieces(w_in, B, S)
    def start_layer(i, rows):
        normed[i], qkv[i] = clock.did(project(clock.now(rows), gain_a, shift_a, w_qkv, bias_qkv))

    def attention(i):
        context[i], lse[i] = clock.did(attend(clock.now(qkv[i]), steps, S))

    def branch_out(i):
        return clock.did(matmul(clock.now(context[i]), w_o, dot_nn, parts_out))

    def middle_of(i, branch):
        middle[i], own_normed = clock.did(
            second_norm(i, clock.now(branch), inputs, active[i], bias_o_full, gain_b, shift_b)
        )
        return own_normed

    def hidden_units(i):
        hidden[i], grad_pre[i], sum_pre[i] = clock.did(
            hidden_both(clock.now(normed_two[i]), grad_hidden[i], w_1, bias_hidden)
        )

    def hidden_back(i):
        grad_hidden[i] = clock.did(matmul(clock.now(grad_branch_two[i]), w_2, dot_nt))

    def normed_two_back(i):
        return clock.did(matmul(clock.now(grad_pre[i]), w_1, dot_nt, parts_out))

    def middle_back(i, back):
        grad_middle[i], own_grad_branch[i], sums_two[i] = clock.did(
            second_norm_back(i, clock.now(back), middle[i], cotangent, active[i], gain_b)
        )

    def context_back(i):
        grad_context[i] = clock.did(matmul(clock.now(grad_branch[i]), w_o, dot_nt))

    def attention_back(i):
        grad_qkv[i] = clock.did(attend_back(qkv[i], clock.now(grad_context[i]), lse[i], steps, S))

    def normed_back(i):
        return clock.did(matmul(clock.now(grad_qkv[i]), w_qkv, dot_nt, parts_out))

    def start_back(i, back):
        input_grad[i], sums_one[i] = clock.did(
            first_norm_back(i, clock.now(back), inputs, grad_middle[i], gain_a, input_grad[i - 1] if i else None)
        )

    def branch_two_out(i):
        return clock.did(matmul(clock.now(hidden[i]), w_2, dot_nn, parts_out))

    def finish(i, branch_two):
        output[i] = clock.did(
            final_sum(i, slots, clock.now(branch_two), middle[i], active[i], bias_out_full, output[i - 1] if i else None)
        )

    def gradient(lefts, rights):
        return clock.did(weight_sum(clock.now(lefts), rights))

    parts_out = ring.parts(T)

    tokens = lambda parts: sum(jnp.sum(p.astype(f32), 0) for p in parts)
    plain = lambda v: v.reshape(devices, r)
    pair_sum = lambda pairs, k: plain(pairs[0][k] + pairs[1][k])

    def own_heads(v):
        if whole_heads:
            spread = jnp.zeros((B, S, r), f32)
            return lax.dynamic_update_slice(spread, v.reshape(B, 1, r), (0, s, 0)).reshape(devices, r)
        return lax.dynamic_update_slice(jnp.zeros((D,), f32), v, (s * Dl,)).reshape(devices, r)

    def early_pack():
        own_hidden = lax.dynamic_update_slice(
            jnp.zeros((B, S, rw), f32), sum(sum_pre).reshape(B, 1, rw), (0, s, 0)
        ).reshape(devices, rw)
        parts = (
            pair_sum(sums_two, 2), pair_sum(sums_two, 0), pair_sum(sums_two, 1), pair_sum(sums_two, 3), own_hidden,
        )
        return jnp.concatenate(parts, -1)

    def late_pack():
        bias_sums = tokens(grad_qkv)
        parts = (
            pair_sum(sums_one, 0), pair_sum(sums_one, 1), own_heads(bias_sums[:Dl]),
            own_heads(bias_sums[2 * Dl :]),
        )
        return jnp.concatenate(parts, -1)

    fresh = lambda: [None] * slots
    normed, qkv, context, lse, middle, normed_two, sums_one, sums_two = (fresh() for _ in range(8))
    hidden, sum_pre, grad_pre, output, grad_middle, grad_branch = (fresh() for _ in range(6))
    own_grad_branch, grad_branch_two, grad_hidden, grad_context, grad_qkv, input_grad = (fresh() for _ in range(6))
    assert slots == 2
    begin, bring = partial(Scatter, ring, clock), partial(Gather, ring, clock)

    qkv_rows = clock.did(ring.swap(qkv_pieces).reshape(S * r, 3 * Dl))
    w_qkv = gather(qkv_rows)
    in_rows = ring.swap(clock.now(in_pieces)).reshape(S * r, Fl)
    in0 = bring(inputs[0])
    in_rows = clock.did(clock.now(in_rows))
    in0.go()
    if whole_heads:
        w_o = gather(clock.now(wo))
    else:
        w_o = lax.all_gather(clock.now(wo), ALL, axis=0, tiled=True)
        w_o = lax.dynamic_slice(w_o, (s * Dl, 0), (Dl, D))
    in1 = bring(inputs[1])

    small = (gain_one, shift_one, bias_q, bias_v, bias_o, gain_two, shift_two, bias_out)
    packed = clock.did(gather_small(clock.now(jnp.concatenate(small + (bias_in,))), devices))
    full = lambda k: packed[:, k * r : (k + 1) * r].reshape(1, D).astype(f32)
    mine = lambda k: (
        lax.dynamic_index_in_dim(packed.reshape(B, S, -1), s, 1, False)[:, k * r : (k + 1) * r]
        if whole_heads
        else lax.dynamic_slice(packed[:, k * r : (k + 1) * r].reshape(D), (s * Dl,), (Dl,))
    ).reshape(Dl).astype(f32)
    gain_a, shift_a, bias_o_full, gain_b, shift_b, bias_out_full = (full(k) for k in (0, 1, 4, 5, 6, 7))
    bias_qkv = jnp.concatenate([mine(2), jnp.zeros((Dl,), f32), mine(3)])[None]
    bias_hidden = (
        lax.dynamic_index_in_dim(packed.reshape(B, S, -1), s, 1, False)[:, len(small) * r :]
        .reshape(1, Fl).astype(f32)
    )

    in0.arrive()
    start_layer(0, in0.result())
    in1.go()
    w_2 = gather(clock.now(w_out))
    cot0 = bring(grad_two[0])
    attention(0)
    in1.arrive()
    br0 = begin(branch_out(0))
    w_1 = gather(clock.now(in_rows))
    start_layer(1, in1.result())
    cot0.go()
    attention(1)
    br0.go()
    cot0.arrive()
    cot1 = bring(grad_two[1])
    br1 = begin(branch_out(1))
    br0.arrive()
    nt0 = bring(middle_of(0, br0.result()))
    br1.go()
    grad_branch_two[0] = cot0.result()
    hidden_back(0)
    nt0.go()
    br1.arrive()
    nt1 = bring(middle_of(1, br1.result()))
    nt0.arrive()
    cot1.go()
    normed_two[0] = nt0.result()
    hidden_units(0)
    nt1.go()
    cot1.arrive()
    grad_branch_two[1] = cot1.result()
    hidden_back(1)
    gn0 = begin(normed_two_back(0))
    nt1.arrive()
    normed_two[1] = nt1.result()
    hidden_units(1)
    gn0.go()
    sum_w_2 = gradient(hidden, grad_branch_two)
    sum_w_2 = scatter(sum_w_2)
    gn0.arrive()
    middle_back(0, gn0.result())
    gb0 = bring(own_grad_branch[0])
    gn1 = begin(normed_two_back(1))
    sum_w_1 = gradient(normed_two, grad_pre)
    gb0.go()
    gn1.go()
    part = branch_two_out(0)
    gb0.arrive()
    out0 = begin(part)
    grad_branch[0] = gb0.result()
    context_back(0)
    gn1.arrive()
    middle_back(1, gn1.result())
    gb1 = bring(own_grad_branch[1])
    early = SmallScatter(clock, early_pack())
    early.step()
    sum_w_1 = scatter(after(clock.now(sum_w_1), sum_w_2))
    attention_back(0)
    gb1.go()
    out0.go()
    early.step()
    gx0 = begin(normed_back(0))
    part = branch_two_out(1)
    gb1.arrive()
    grad_branch[1] = gb1.result()
    context_back(1)
    out0.arrive()
    gx0.go()
    early.step()
    sum_o = gradient(context, grad_branch)
    if whole_heads:
        sum_o = scatter(after(clock.now(sum_o), sum_w_1))
    else:
        sum_o = lax.dynamic_update_slice(jnp.zeros((D, D), bf16), sum_o, (s * Dl, 0))
        sum_o = lax.psum_scatter(sum_o, ALL, scatter_dimension=0, tiled=True)
    out1 = begin(part)
    attention_back(1)
    gx0.arrive()
    out1.go()
    gx1 = begin(normed_back(1))
    sum_qkv = gradient(normed, grad_qkv)
    sum_qkv = scatter(after(clock.now(sum_qkv), sum_o))
    gx1.go()
    early.step()
    start_back(0, gx0.result())
    finish(0, out0.result())
    out1.arrive()
    finish(1, out1.result())
    sum_w_1 = ring.swap(clock.now(sum_w_1).reshape(S, r, Fl))
    gx1.arrive()
    start_back(1, gx1.result())
    sum_w_1 = clock.did(unit_rows(clock.now(sum_w_1), B))
    late = SmallScatter(clock, late_pack())
    early, late = early.result(), late.result()
    clock.did(late)

    sum_qkv = ring.swap(clock.now(sum_qkv).reshape(S, r, 3 * Dl))
    if whole_heads:
        sum_q, sum_k, sum_v = head_rows(sum_qkv, B)
    else:
        sum_q, sum_k, sum_v = (
            sum_qkv[:, :, c * Dl : (c + 1) * Dl].transpose(1, 0, 2).reshape(r, D) for c in range(3)
        )

    bo, g2, s2, b2 = (early[k * r : (k + 1) * r] for k in range(4))
    g1, s1, bq, bv = (late[k * r : (k + 1) * r] for k in range(4))
    wide = lambda v: v.astype(f32)
    return (
        output[-1], input_grad[-1], wide(sum_q), wide(sum_k), wide(sum_v), wide(sum_o),
        g1, s1, bq, bv, bo, sum_w_1, wide(sum_w_2), g2, s2, early[4 * r :], b2,
    )


def solution(mesh):
    tokens, rows, vector = P("batch", "seq", None), P(ALL, None), P(ALL)
    placed = (
        (tokens, tokens, P("batch"), P("batch"), P())
        + (rows,) * 4 + (vector,) * 5 + (rows,) * 2 + (vector,) * 4
    )
    out = (tokens, tokens) + (rows,) * 4 + (vector,) * 5 + (rows,) * 2 + (vector,) * 4
    return jax.shard_map(body, mesh=mesh, in_specs=placed, out_specs=out, check_vma=False)
```

```python
from functools import partial

import jax
import jax.numpy as jnp
import numpy as np
from jax import lax
from jax.experimental import pallas as pl
from jax.experimental.pallas import tpu as pltpu
from jax.sharding import PartitionSpec as P

HEAD_DIM = 64
PAIR = 2 * HEAD_DIM
epsilon = 1e-05
LOG2E = 1.4426950408889634
bf16, f32 = jnp.bfloat16, jnp.float32
ALL = ("batch", "seq")
VMEM_LIMIT = 56 * 1024 * 1024


def dot_nn(a, b):
    return jnp.dot(a, b, preferred_element_type=f32)


def dot_nt(a, b):
    return lax.dot_general(a, b, (((1,), (1,)), ((), ())), preferred_element_type=f32)


def dot_tn(a, b):
    return lax.dot_general(a, b, (((0,), (0,)), ((), ())), preferred_element_type=f32)


PARAMS = pltpu.CompilerParams(vmem_limit_bytes=VMEM_LIMIT)
PACE = 0.5


def cost(flops):
    return pl.CostEstimate(flops=int(PACE * flops), bytes_accessed=int(PACE * flops / 320), transcendentals=0)


def tile_of(width, most=512):
    return next(t for t in (most, 256, 128, width) if width % t == 0)


def listed(value):
    return list(value) if isinstance(value, (list, tuple)) else [value]


def rows_of(pieces):
    return sum(p.shape[0] for p in pieces)


def fixed(shape):
    return pl.BlockSpec(shape, lambda j: (0,) * len(shape))


def join(refs, whole):
    at = 0
    for ref in refs:
        whole[at : at + ref.shape[0], :] = ref[...]
        at += ref.shape[0]


def first_step(body):
    pl.when(pl.program_id(0) == 0)(body)


def matmul(left, right, dot, parts=None):
    left = listed(left)
    n, rows, depth = len(left), rows_of(left), left[0].shape[1]
    width = right.shape[1] if dot is dot_nn else right.shape[0]
    tile, ranges = tile_of(width), parts or [[(0, rows)]]
    sizes = [sum(stop - begin for begin, stop in part) for part in ranges]

    def kernel(*refs):
        whole = refs[0]
        if n > 1:
            whole = refs[-1]
            first_step(lambda: join(refs[:n], whole))
        total = dot(whole[...], refs[n][...]).astype(bf16)
        for ref, part in zip(refs[n + 1 :], ranges):
            at = 0
            for begin, stop in part:
                ref[at : at + stop - begin, :] = total[begin:stop]
                at += stop - begin

    strip = (
        pl.BlockSpec((depth, tile), lambda j: (0, j)) if dot is dot_nn else pl.BlockSpec((tile, depth), lambda j: (j, 0))
    )
    out = pl.pallas_call(
        kernel,
        out_shape=tuple(jax.ShapeDtypeStruct((size, width), bf16) for size in sizes),
        grid=(width // tile,),
        in_specs=[fixed(p.shape) for p in left] + [strip],
        out_specs=tuple(pl.BlockSpec((size, tile), lambda j: (0, j)) for size in sizes),
        scratch_shapes=[pltpu.VMEM((rows, depth), bf16)] if n > 1 else [],
        compiler_params=PARAMS, cost_estimate=cost(3.5 * rows * depth * width), name="matmul",
    )(*left, right)
    return out if parts else out[0]


def weight_sum(lefts, rights):
    lefts, rights = [listed(v) for v in lefts], [listed(v) for v in rights]
    tokens = [rows_of(v) for v in lefts]
    rows, width = lefts[0][0].shape[1], rights[0][0].shape[1]
    tile = tile_of(rows, 256)
    sizes = [len(v) for v in lefts + rights]
    spots = [pltpu.VMEM((t, tile), bf16) for t in tokens] + [pltpu.VMEM((t, width), bf16) for t in tokens]
    spots = [spot if size > 1 else pltpu.VMEM((16, 128), bf16) for spot, size in zip(spots, sizes)]
    n = len(lefts)

    def kernel(*refs):
        out, spot, at, wholes = refs[sum(sizes)], refs[sum(sizes) + 1 :], 0, []
        for k, size in enumerate(sizes):
            group = refs[at : at + size]
            at += size
            if size == 1:
                wholes.append(group[0])
                continue
            wholes.append(spot[k])
            if k < n:
                join(group, spot[k])
            else:
                first_step(partial(join, group, spot[k]))
        total = sum(dot_tn(wholes[k][...], wholes[n + k][...]) for k in range(n))
        out[...] = total.astype(bf16)

    return pl.pallas_call(
        kernel,
        out_shape=jax.ShapeDtypeStruct((rows, width), bf16),
        grid=(rows // tile,),
        in_specs=[pl.BlockSpec((p.shape[0], tile), lambda j: (0, j)) for v in lefts for p in v]
        + [fixed(p.shape) for v in rights for p in v],
        out_specs=pl.BlockSpec((tile, width), lambda j: (j, 0)),
        scratch_shapes=spots,
        compiler_params=PARAMS, cost_estimate=cost(3.3 * sum(tokens) * rows * width), name="weight_sum",
    )(*(p for v in lefts + rights for p in v))


def norm_parts(rows):
    centered = rows - jnp.mean(rows, -1, keepdims=True)
    spread = jnp.mean(centered * centered, -1, keepdims=True)
    inverse = lax.rsqrt(spread + epsilon)
    return centered * inverse, inverse


def norm_back(grad, gain, unit, inverse):
    scaled = grad * gain
    return inverse * (
        scaled - jnp.mean(scaled, -1, keepdims=True) - unit * jnp.mean(scaled * unit, -1, keepdims=True)
    )


def project(pieces, gain, shift, w_qkv, bias):
    n, rows, (depth, width) = len(pieces), rows_of(pieces), w_qkv.shape
    tile = tile_of(width)

    def kernel(*refs):
        gain_ref, shift_ref, w_ref, bias_ref, normed, out = refs[n:]

        def norm():
            at = 0
            for ref in refs[:n]:
                for k in range(0, ref.shape[0], 64):
                    unit, _ = norm_parts(ref[k : k + 64, :].astype(f32))
                    normed[at + k : at + k + 64, :] = (unit * gain_ref[...] + shift_ref[...]).astype(bf16)
                at += ref.shape[0]

        first_step(norm)
        out[...] = (dot_nn(normed[...], w_ref[...]) + bias_ref[...]).astype(bf16)

    return pl.pallas_call(
        kernel,
        out_shape=(jax.ShapeDtypeStruct((rows, depth), bf16), jax.ShapeDtypeStruct((rows, width), bf16)),
        grid=(width // tile,),
        in_specs=[fixed(p.shape) for p in pieces]
        + [fixed((1, depth)), fixed((1, depth)), pl.BlockSpec((depth, tile), lambda j: (0, j)), pl.BlockSpec((1, tile), lambda j: (0, j))],
        out_specs=(fixed((rows, depth)), pl.BlockSpec((rows, tile), lambda j: (0, j))),
        compiler_params=PARAMS, cost_estimate=cost(5 * rows * depth * width), name="project",
    )(*pieces, gain, shift, w_qkv, bias)


def gelu_both(pre):
    below = 0.5 * (1.0 + lax.erf(pre * (0.5**0.5)))
    density = jnp.exp(-0.5 * pre * pre) * ((2.0 * np.pi) ** -0.5)
    return pre * below, below + pre * density


def hidden_both(normed, grad_hidden, w_1, bias):
    n, rows, (depth, width) = len(normed), rows_of(normed), w_1.shape
    tile = tile_of(width)

    def kernel(*refs):
        g_ref, w1_ref, b_ref, h_ref, p_ref, s_ref, whole = refs[n:]
        first_step(lambda: join(refs[:n], whole))
        value, slope = gelu_both(dot_nn(whole[...], w1_ref[...]) + b_ref[...])
        h_ref[...] = value.astype(bf16)
        grad_pre = (g_ref[...].astype(f32) * slope).astype(bf16)
        p_ref[...] = grad_pre
        s_ref[...] = jnp.sum(grad_pre.astype(f32), 0, keepdims=True)

    part = pl.BlockSpec((rows, tile), lambda j: (0, j))
    line = pl.BlockSpec((1, tile), lambda j: (0, j))
    return pl.pallas_call(
        kernel,
        out_shape=(jax.ShapeDtypeStruct((rows, width), bf16),) * 2 + (jax.ShapeDtypeStruct((1, width), f32),),
        grid=(width // tile,),
        in_specs=[fixed(p.shape) for p in normed] + [part, pl.BlockSpec((depth, tile), lambda j: (0, j)), line],
        out_specs=(part, part, line),
        scratch_shapes=[pltpu.VMEM((rows, depth), bf16)],
        compiler_params=PARAMS, cost_estimate=cost(5 * rows * depth * width), name="hidden_both",
    )(*normed, grad_hidden, w_1, bias)


STEP = 64


def own_rows(depth):
    return pl.BlockSpec((STEP, depth), lambda j: (j, 0))


def slot_rows(slot, depth):
    return pl.BlockSpec((1, STEP, depth), lambda j: (slot, j, 0))


def summed_rows(rows, depth):
    half = rows // 2 // STEP
    spec = lambda place: pl.BlockSpec((STEP, depth), lambda j: (place(j), 0))
    return [
        own_rows(depth), spec(lambda j: jnp.maximum(j, half)), spec(lambda j: jnp.minimum(j, half - 1) + half),
        spec(lambda j: jnp.minimum(j, half - 1)), spec(lambda j: jnp.maximum(j - half, 0)),
    ]


def summed(refs, steps):
    own, up, down, far_up, far_down = (ref[...].astype(f32) for ref in refs)
    early = pl.program_id(0) < steps // 2
    return own + jnp.where(early, far_up, up) + jnp.where(early, down, far_down)


def second_norm(slot, branch, inputs, active, bias, gain, shift):
    rows, depth = branch[0].shape

    def kernel(*refs):
        x, act, bias_ref, gain_ref, shift_ref, middle, normed = refs[5:]
        total = summed(refs[:5], rows // STEP) + bias_ref[...]
        total = x[0].astype(f32) + act[...] * total
        middle[...] = total
        normed[...] = (norm_parts(total)[0] * gain_ref[...] + shift_ref[...]).astype(bf16)

    return pl.pallas_call(
        kernel,
        out_shape=(jax.ShapeDtypeStruct((rows, depth), f32), jax.ShapeDtypeStruct((rows, depth), bf16)),
        grid=(rows // STEP,),
        in_specs=summed_rows(rows, depth) + [slot_rows(slot, depth), own_rows(1)] + [fixed((1, depth))] * 3,
        out_specs=(own_rows(depth), own_rows(depth)),
        compiler_params=PARAMS, cost_estimate=cost(6e9), name="second_norm",
    )(*branch, inputs, active, bias, gain, shift)


def add_line(sums, line, value):
    sums[line : line + 1, :] += jnp.sum(value, 0, keepdims=True)


def second_norm_back(slot, back, middle, cotangent, active, gain):
    rows, depth = middle.shape

    def kernel(*refs):
        mid, cot, act, gain_ref, grad_middle, grad_branch, sums = refs[5:]

        @first_step
        def _():
            sums[...] = jnp.zeros_like(sums)

        grad = summed(refs[:5], rows // STEP)
        unit, inverse = norm_parts(mid[...])
        outer = cot[0].astype(f32)
        total = outer + norm_back(grad, gain_ref[...], unit, inverse)
        grad_middle[...] = total
        branch = (act[...] * total).astype(bf16)
        grad_branch[...] = branch
        add_line(sums, 0, grad * unit)
        add_line(sums, 1, grad)
        add_line(sums, 2, branch.astype(f32))
        add_line(sums, 3, (act[...] * outer).astype(bf16).astype(f32))

    return pl.pallas_call(
        kernel,
        out_shape=(
            jax.ShapeDtypeStruct((rows, depth), f32), jax.ShapeDtypeStruct((rows, depth), bf16),
            jax.ShapeDtypeStruct((8, depth), f32),
        ),
        grid=(rows // STEP,),
        in_specs=summed_rows(rows, depth) + [own_rows(depth), slot_rows(slot, depth), own_rows(1), fixed((1, depth))],
        out_specs=(own_rows(depth), own_rows(depth), fixed((8, depth))),
        compiler_params=PARAMS, cost_estimate=cost(7e9), name="second_norm_back",
    )(*back, middle, cotangent, active, gain)


def first_norm_back(slot, back, inputs, grad_middle, gain, others):
    (rows, depth), slots = grad_middle.shape, inputs.shape[0]
    more = [] if others is None else [others]

    def kernel(*refs):
        x, grad_mid, gain_ref = refs[5:8]
        out, sums = refs[-2:]

        @first_step
        def _():
            sums[...] = jnp.zeros_like(sums)

        grad = summed(refs[:5], rows // STEP)
        unit, inverse = norm_parts(x[0].astype(f32))
        out[0] = (grad_mid[...] + norm_back(grad, gain_ref[...], unit, inverse)).astype(bf16)
        add_line(sums, 0, grad * unit)
        add_line(sums, 1, grad)

    return pl.pallas_call(
        kernel,
        out_shape=(jax.ShapeDtypeStruct((slots, rows, depth), bf16), jax.ShapeDtypeStruct((8, depth), f32)),
        grid=(rows // STEP,),
        in_specs=summed_rows(rows, depth) + [slot_rows(slot, depth), own_rows(depth), fixed((1, depth))]
        + [pl.BlockSpec(memory_space=pl.ANY)] * len(more),
        out_specs=(slot_rows(slot, depth), fixed((8, depth))),
        input_output_aliases={8: 0} if more else {},
        compiler_params=PARAMS, cost_estimate=cost(7e9), name="first_norm_back",
    )(*back, inputs, grad_middle, gain, *more)


def final_sum(slot, slots, branch, middle, active, bias, others):
    rows, depth = middle.shape
    more = [] if others is None else [others]

    def kernel(*refs):
        mid, act, bias_ref = refs[5:8]
        total = summed(refs[:5], rows // STEP) + bias_ref[...]
        refs[-1][0] = (mid[...] + act[...] * total).astype(bf16)

    return pl.pallas_call(
        kernel,
        out_shape=jax.ShapeDtypeStruct((slots, rows, depth), bf16),
        grid=(rows // STEP,),
        in_specs=summed_rows(rows, depth) + [own_rows(depth), own_rows(1), fixed((1, depth))] + [pl.BlockSpec(memory_space=pl.ANY)] * len(more),
        out_specs=slot_rows(slot, depth),
        input_output_aliases={8: 0} if more else {},
        compiler_params=PARAMS, cost_estimate=cost(6e9), name="final_sum",
    )(*branch, middle, active, bias, *more)


def head_pieces(weights, groups, blocks):
    rows = weights[0].shape[0]

    def kernel(*refs):
        for k in range(blocks):
            strips = [ref[:, (g * blocks + k) * rows : (g * blocks + k + 1) * rows] for ref in refs[:-1] for g in range(groups)]
            refs[-1][k] = jnp.concatenate(strips, 1)

    return pl.pallas_call(
        kernel,
        out_shape=jax.ShapeDtypeStruct((blocks, rows, 3 * groups * rows), bf16),
        compiler_params=PARAMS, cost_estimate=cost(2e9), name="head_pieces",
    )(*weights)


def unit_pieces(weight, groups, blocks):
    (rows, width), n = weight.shape, weight.shape[1] // (groups * blocks)

    def kernel(ref, out):
        for k in range(blocks):
            for g in range(groups):
                out[k, :, g * n : (g + 1) * n] = ref[:, (g * blocks + k) * n : (g * blocks + k + 1) * n]

    return pl.pallas_call(
        kernel,
        out_shape=jax.ShapeDtypeStruct((blocks, rows, groups * n), bf16),
        compiler_params=PARAMS, cost_estimate=cost(2e9), name="unit_pieces",
    )(weight) if n % 128 == 0 else weight.reshape(rows, groups, blocks, n).transpose(2, 0, 1, 3).reshape(blocks, rows, groups * n)


def unit_rows(pieces, groups):
    blocks, rows, width = pieces.shape
    n = width // groups

    def kernel(ref, out):
        for k in range(blocks):
            for g in range(groups):
                out[:, (g * blocks + k) * n : (g * blocks + k + 1) * n] = ref[k, :, g * n : (g + 1) * n].astype(f32)

    return pl.pallas_call(
        kernel,
        out_shape=jax.ShapeDtypeStruct((rows, blocks * width), f32),
        compiler_params=PARAMS, cost_estimate=cost(2e9), name="unit_rows",
    )(pieces) if n % 128 == 0 else pieces.reshape(blocks, rows, groups, n).transpose(1, 2, 0, 3).reshape(rows, -1).astype(f32)


def head_rows(pieces, groups):
    blocks, rows, width = pieces.shape

    def kernel(ref, *outs):
        for c, out in enumerate(outs):
            strips = [
                ref[k, :, (c * groups + g) * rows : (c * groups + g + 1) * rows] for g in range(groups) for k in range(blocks)
            ]
            out[...] = jnp.concatenate(strips, 1).astype(f32)

    return pl.pallas_call(
        kernel,
        out_shape=(jax.ShapeDtypeStruct((rows, blocks * width // 3), f32),) * 3,
        compiler_params=PARAMS, cost_estimate=cost(2e9), name="head_rows",
    )(pieces)


def after(value, others):
    return value if others is None else lax.optimization_barrier((value, others))[0]


class Clock:
    def __init__(self):
        self.last = None

    def now(self, value):
        return after(value, self.last)

    def did(self, value):
        self.last = jax.tree.leaves(value)
        return value


class Ring:
    def __init__(self, size):
        self.size = size
        self.order = [i ^ (i >> 1) for i in range(size)]
        self.place = [self.order.index(i) for i in range(size)]

    def parts(self, rows):
        n, half = self.size, rows // 2
        first = lambda k: (k * rows, k * rows + half)
        second = lambda k: (k * rows + half, (k + 1) * rows)
        far = n // 2
        out = [[(0, rows)], [first(far), second(far - 1)], [second(far), first(far + 1)]]
        for k in range(far - 1, 1, -1):
            out += [[first(k)], [second(k - 1)], [second(n - k)], [first(n - k + 1)]]
        return out + [[first(1)], [second(n - 1)]]

    def send(self, value, steps):
        n = self.size
        return lax.ppermute(value, "seq", [(self.order[i], self.order[(i + steps) % n]) for i in range(n)])

    def mine(self):
        place, shift = lax.axis_index("seq"), 1
        while shift < self.size:
            place = place ^ (place >> shift)
            shift *= 2
        return place

    def at(self, steps):
        place = (self.mine() + steps) & (self.size - 1)
        return place ^ (place >> 1)

    def steps_to(self):
        return (jnp.array(self.place, jnp.int32) - self.mine()) & (self.size - 1)

    def swap(self, pieces):
        take = lambda k: lax.dynamic_slice_in_dim(pieces, self.at(k), 1)
        out = lax.dynamic_update_slice_in_dim(jnp.zeros_like(pieces), take(0), self.at(0), 0)
        for k in range(1, self.size):
            came = self.send(take(k), k)
            out = lax.dynamic_update_slice_in_dim(out, came, self.at(-k), 0)
        return out


class Gather:
    def __init__(self, ring, clock, block):
        self.ring, self.clock = ring, clock
        self.half = block.shape[0] // 2
        self.near, self.far = [block], []
        block = clock.now(block)
        self.rising, self.falling = ring.send(block, 1), ring.send(block, -1)

    def go(self):
        ring = self.ring
        for _ in range(2, ring.size // 2):
            self.far.append(self.rising)
            self.near.append(self.falling)
            self.rising, self.falling = ring.send(self.rising, 1), ring.send(self.falling, -1)
        rising, falling = self.clock.did(self.clock.now((self.rising, self.falling)))
        self.far.append(rising)
        self.near.append(falling)
        first, second = self.clock.did((rising[: self.half], falling[self.half :]))
        self.middle = [ring.send(first, 1), ring.send(second, -1)]

    def arrive(self):
        self.middle = list(self.clock.did(self.clock.now(tuple(self.middle))))

    def result(self):
        return self.clock.now(self.near + self.middle + self.far[::-1])


class Scatter:
    def __init__(self, ring, clock, part):
        self.ring, self.clock, self.part = ring, clock, part
        self.up, self.down = ring.send(part[1], 1), ring.send(part[2], -1)

    def go(self):
        n, send, now, did = self.ring.size, self.ring.send, self.clock.now, self.clock.did
        half = self.part[1].shape[0] // 2
        rest = self.part[3:]
        for k in range(0, 4 * (n // 2 - 2), 4):
            up = jnp.concatenate([add16(rest[k], self.up[:half]), add16(rest[k + 1], self.up[half:])])
            down = jnp.concatenate([add16(rest[k + 2], self.down[:half]), add16(rest[k + 3], self.down[half:])])
            self.up, self.down = send(up, 1), send(down, -1)
        up, down = did(now((self.up, self.down)))
        far_up, far_down = did((add16(rest[-2], up[:half]), add16(rest[-1], down[:half])))
        self.up, self.down = up, down
        self.far_up, self.far_down = send(far_up, 1), send(far_down, -1)

    def arrive(self):
        self.far_up, self.far_down = self.clock.did(self.clock.now((self.far_up, self.far_down)))

    def result(self):
        return (self.part[0], self.up, self.down) + self.clock.now((self.far_up, self.far_down))


def add16(a, b):
    return (a.astype(f32) + b.astype(f32)).astype(bf16)


def gather_small(block, devices):
    place = lax.axis_index(ALL)
    have, bit = block[None], 1
    while bit < devices:
        other = lax.ppermute(have, ALL, [(i, i ^ bit) for i in range(devices)])
        low = (place & bit) == 0
        have = jnp.concatenate([jnp.where(low, have, other), jnp.where(low, other, have)])
        bit *= 2
    return have


class SmallScatter:
    def __init__(self, clock, total):
        self.clock, self.keep, self.came, self.devices = clock, total, None, total.shape[0]

    def gathered(self):
        total = self.clock.now(self.keep)
        return total if self.came is None else self.clock.did(total + self.clock.now(self.came))

    def step(self):
        bit = self.keep.shape[0] // 2
        if bit == 0:
            return
        total = self.gathered()
        low = (lax.axis_index(ALL) & bit) == 0
        self.keep = jnp.where(low, total[:bit], total[bit:])
        send = jnp.where(low, total[bit:], total[:bit])
        self.came = lax.ppermute(send, ALL, [(i, i ^ bit) for i in range(self.devices)])

    def result(self):
        while self.keep.shape[0] > 1:
            self.step()
        return self.gathered()[0]


def attend_kernel(blocks, rows, steps, q_ref, k_ref, v_ref, o_ref, lse_ref, keys, values_t):
    for a in range(blocks):
        here = pl.ds(pl.multiple_of(steps[a] * rows, rows), rows)
        keys[a * rows : (a + 1) * rows, :] = k_ref[here, :]
        values_t[:, a * rows : (a + 1) * rows] = v_ref[here, :].astype(f32).T.astype(bf16)
    lane = lax.broadcasted_iota(jnp.int32, (1, PAIR), 1)
    causal = lax.broadcasted_iota(jnp.int32, (rows, rows), 0) <= lax.broadcasted_iota(
        jnp.int32, (rows, rows), 1
    )
    scale = HEAD_DIM ** (-0.5) * LOG2E
    for i in range(blocks):
        here = pl.ds(pl.multiple_of(steps[i] * rows, rows), rows)
        query = q_ref[here, :]
        ahead = i * rows
        parts = []
        for head in range(2):
            own = (lane // HEAD_DIM == head).astype(bf16)
            lines = slice(head * HEAD_DIM, (head + 1) * HEAD_DIM)
            q_head = query * own
            diag = dot_nt(keys[ahead : ahead + rows, :], q_head) * scale
            diag = jnp.where(causal, diag, -1e30)
            top = jnp.max(diag, 0, keepdims=True)
            if i > 0:
                full = dot_nt(keys[:ahead, :], q_head) * scale
                top = jnp.maximum(top, jnp.max(full, 0, keepdims=True))
            diag = jnp.exp2(diag - top)
            total = jnp.sum(diag, 0, keepdims=True)
            mixed = dot_nn(values_t[lines, ahead : ahead + rows], diag.astype(bf16))
            if i > 0:
                full = jnp.exp2(full - top)
                total = total + jnp.sum(full, 0, keepdims=True)
                mixed = mixed + dot_nn(values_t[lines, :ahead], full.astype(bf16))
            parts.append(mixed / total)
            lse_ref[0, head : head + 1, ahead : ahead + rows] = top + jnp.log2(total)
        o_ref[here, :] = jnp.concatenate(parts).T.astype(bf16)


def attend(qkv, steps, blocks):
    tokens, width = qkv.shape[0], qkv.shape[1] // 3
    pairs, rows = width // PAIR, tokens // blocks
    column = lambda c: pl.BlockSpec((tokens, PAIR), lambda h, steps: (0, c * pairs + h))
    return pl.pallas_call(
        partial(attend_kernel, blocks, rows),
        out_shape=(
            jax.ShapeDtypeStruct((tokens, width), bf16),
            jax.ShapeDtypeStruct((pairs, 2, tokens), f32),
        ),
        grid_spec=pltpu.PrefetchScalarGridSpec(
            num_scalar_prefetch=1,
            grid=(pairs,),
            in_specs=[column(0), column(1), column(2)],
            out_specs=(column(0), pl.BlockSpec((1, 2, tokens), lambda h, steps: (h, 0, 0))),
            scratch_shapes=[pltpu.VMEM((tokens, PAIR), bf16), pltpu.VMEM((PAIR, tokens), bf16)],
        ),
        compiler_params=pltpu.CompilerParams(vmem_limit_bytes=VMEM_LIMIT),
        cost_estimate=cost(32 * tokens * tokens * width),
        name="attend",
    )(steps, qkv, qkv, qkv)


def attend_back_kernel(
    blocks, rows, steps, q_ref, k_ref, v_ref, g_ref, lse_ref, d_ref, keys, keys_t, values, dk, dv, dk16, dv16
):
    @pl.when(pl.program_id(1) == 0)
    def _():
        for a in range(blocks):
            here = pl.ds(pl.multiple_of(steps[a] * rows, rows), rows)
            place = slice(a * rows, (a + 1) * rows)
            keys[place, :] = k_ref[here, :]
            keys_t[:, place] = k_ref[here, :].astype(f32).T.astype(bf16)
            values[place, :] = v_ref[here, :]
        dk[...] = jnp.zeros_like(dk)
        dv[...] = jnp.zeros_like(dv)
        lane = lax.broadcasted_iota(jnp.int32, (1, PAIR), 1)
        scaling = HEAD_DIM ** (-0.5)
        for i in range(blocks):
            here = pl.ds(pl.multiple_of(steps[i] * rows, rows), rows)
            query, grad = q_ref[here, :], g_ref[here, :]
            length = (i + 1) * rows
            causal = lax.broadcasted_iota(jnp.int32, (length, rows), 0) <= (
                lax.broadcasted_iota(jnp.int32, (length, rows), 1) + i * rows
            )
            parts = []
            for head in range(2):
                own = (lane // HEAD_DIM == head).astype(bf16)
                lines = slice(head * HEAD_DIM, (head + 1) * HEAD_DIM)
                q_head, g_head = query * own, grad * own
                lse = lse_ref[0, head : head + 1, i * rows : (i + 1) * rows]
                logits = dot_nt(keys[:length, :], q_head) * (scaling * LOG2E)
                probs = jnp.where(causal, jnp.exp2(logits - lse), 0.0)
                grad_probs = dot_nt(values[:length, :], g_head)
                inner = jnp.sum(grad_probs * probs, 0, keepdims=True)
                grad_raw = (probs * (grad_probs - inner) * scaling).astype(bf16)
                parts.append(dot_nn(keys_t[lines, :length], grad_raw))
                dk[:length, :] += dot_nn(grad_raw, q_head)
                dv[:length, :] += dot_nn(probs.astype(bf16), g_head)
            d_ref[here, :] = jnp.concatenate(parts).T.astype(bf16)
        for a in range(blocks):
            here = pl.ds(pl.multiple_of(steps[a] * rows, rows), rows)
            dk16[here, :] = dk[a * rows : (a + 1) * rows, :].astype(bf16)
            dv16[here, :] = dv[a * rows : (a + 1) * rows, :].astype(bf16)

    @pl.when(pl.program_id(1) == 1)
    def _():
        d_ref[...] = dk16[...]

    @pl.when(pl.program_id(1) == 2)
    def _():
        d_ref[...] = dv16[...]


def attend_back(qkv, grad_context, lse, steps, blocks):
    tokens, width = grad_context.shape
    pairs, rows = width // PAIR, tokens // blocks
    column = lambda c: pl.BlockSpec((tokens, PAIR), lambda h, c_out, steps: (0, c * pairs + h))
    wide = lambda dtype: pltpu.VMEM((tokens, PAIR), dtype)
    return pl.pallas_call(
        partial(attend_back_kernel, blocks, rows),
        out_shape=jax.ShapeDtypeStruct((tokens, 3 * width), bf16),
        grid_spec=pltpu.PrefetchScalarGridSpec(
            num_scalar_prefetch=1,
            grid=(pairs, 3),
            in_specs=[
                column(0), column(1), column(2), column(0),
                pl.BlockSpec((1, 2, tokens), lambda h, c_out, steps: (h, 0, 0)),
            ],
            out_specs=pl.BlockSpec((tokens, PAIR), lambda h, c_out, steps: (0, c_out * pairs + h)),
            scratch_shapes=[
                wide(bf16), pltpu.VMEM((PAIR, tokens), bf16), wide(bf16),
                wide(f32), wide(f32), wide(bf16), wide(bf16),
            ],
        ),
        compiler_params=pltpu.CompilerParams(vmem_limit_bytes=VMEM_LIMIT),
        cost_estimate=cost(64 * tokens * tokens * width),
        name="attend_back",
    )(steps, qkv, qkv, qkv, grad_context, lse)


def body(
    inputs, cotangent, max_exit, min_exit, layer, wq, wk, wv, wo, gain_one, shift_one, bias_q, bias_v,
    bias_o, w_in, w_out, gain_two, shift_two, bias_in, bias_out,
):
    B, S = lax.axis_size("batch"), lax.axis_size("seq")
    devices = B * S
    s = lax.axis_index("seq")
    slots, T, D = inputs.shape
    r, rw = wq.shape[0], w_out.shape[0]
    Dl, Fl = D // S, rw * B
    whole_heads = r % HEAD_DIM == 0
    ring = Ring(S)
    steps = ring.steps_to()

    places = s * T + jnp.arange(T, dtype=jnp.int32)
    exits = max_exit[:, None] - (max_exit - min_exit)[:, None] * places[None, :] // (S * T - 1)
    active = (layer[0] < exits).astype(f32)[..., None]

    clock = Clock()
    grad_two = [(active[i] * cotangent[i].astype(f32)).astype(bf16) for i in range(slots)]
    gather = lambda x: lax.all_gather(x, "batch", axis=0, tiled=True)
    scatter = lambda x: lax.psum_scatter(x, "batch", scatter_dimension=0, tiled=True)
    qkv_pieces = (
        head_pieces((wq, wk, wv), B, S)
        if whole_heads
        else jnp.concatenate([w.reshape(r, S, Dl).transpose(1, 0, 2) for w in (wq, wk, wv)], -1)
    )
    in_pieces = unit_pieces(w_in, B, S)
    def start_layer(i, rows):
        normed[i], qkv[i] = clock.did(project(clock.now(rows), gain_a, shift_a, w_qkv, bias_qkv))

    def attention(i):
        context[i], lse[i] = clock.did(attend(clock.now(qkv[i]), steps, S))

    def branch_out(i):
        return clock.did(matmul(clock.now(context[i]), w_o, dot_nn, parts_out))

    def middle_of(i, branch):
        middle[i], own_normed = clock.did(
            second_norm(i, clock.now(branch), inputs, active[i], bias_o_full, gain_b, shift_b)
        )
        return own_normed

    def hidden_units(i):
        hidden[i], grad_pre[i], sum_pre[i] = clock.did(
            hidden_both(clock.now(normed_two[i]), grad_hidden[i], w_1, bias_hidden)
        )

    def hidden_back(i):
        grad_hidden[i] = clock.did(matmul(clock.now(grad_branch_two[i]), w_2, dot_nt))

    def normed_two_back(i):
        return clock.did(matmul(clock.now(grad_pre[i]), w_1, dot_nt, parts_out))

    def middle_back(i, back):
        grad_middle[i], own_grad_branch[i], sums_two[i] = clock.did(
            second_norm_back(i, clock.now(back), middle[i], cotangent, active[i], gain_b)
        )

    def context_back(i):
        grad_context[i] = clock.did(matmul(clock.now(grad_branch[i]), w_o, dot_nt))

    def attention_back(i):
        grad_qkv[i] = clock.did(attend_back(qkv[i], clock.now(grad_context[i]), lse[i], steps, S))

    def normed_back(i):
        return clock.did(matmul(clock.now(grad_qkv[i]), w_qkv, dot_nt, parts_out))

    def start_back(i, back):
        input_grad[i], sums_one[i] = clock.did(
            first_norm_back(i, clock.now(back), inputs, grad_middle[i], gain_a, input_grad[i - 1] if i else None)
        )

    def branch_two_out(i):
        return clock.did(matmul(clock.now(hidden[i]), w_2, dot_nn, parts_out))

    def finish(i, branch_two):
        output[i] = clock.did(
            final_sum(i, slots, clock.now(branch_two), middle[i], active[i], bias_out_full, output[i - 1] if i else None)
        )

    def gradient(lefts, rights):
        return clock.did(weight_sum(clock.now(lefts), rights))

    parts_out = ring.parts(T)

    tokens = lambda parts: sum(jnp.sum(p.astype(f32), 0) for p in parts)
    plain = lambda v: v.reshape(devices, r)
    pair_sum = lambda pairs, k: plain(pairs[0][k] + pairs[1][k])

    def own_heads(v):
        if whole_heads:
            spread = jnp.zeros((B, S, r), f32)
            return lax.dynamic_update_slice(spread, v.reshape(B, 1, r), (0, s, 0)).reshape(devices, r)
        return lax.dynamic_update_slice(jnp.zeros((D,), f32), v, (s * Dl,)).reshape(devices, r)

    def small_pack():
        own_hidden = lax.dynamic_update_slice(
            jnp.zeros((B, S, rw), f32), sum(sum_pre).reshape(B, 1, rw), (0, s, 0)
        ).reshape(devices, rw)
        parts = (
            pair_sum(sums_two, 2), pair_sum(sums_two, 0), pair_sum(sums_two, 1), pair_sum(sums_two, 3),
            own_heads(bias_sums[:Dl]), own_heads(bias_sums[2 * Dl :]), own_hidden,
        )
        last = pair_sum(sums_one, 0), pair_sum(sums_one, 1)
        return jnp.concatenate(last + parts, -1)

    fresh = lambda: [None] * slots
    normed, qkv, context, lse, middle, normed_two, sums_one, sums_two = (fresh() for _ in range(8))
    hidden, sum_pre, grad_pre, output, grad_middle, grad_branch = (fresh() for _ in range(6))
    own_grad_branch, grad_branch_two, grad_hidden, grad_context, grad_qkv, input_grad = (fresh() for _ in range(6))
    assert slots == 2
    begin, bring = partial(Scatter, ring, clock), partial(Gather, ring, clock)

    qkv_rows = clock.did(ring.swap(qkv_pieces).reshape(S * r, 3 * Dl))
    w_qkv = gather(qkv_rows)
    in_rows = ring.swap(clock.now(in_pieces)).reshape(S * r, Fl)
    in0 = bring(inputs[0])
    in_rows = clock.did(clock.now(in_rows))
    in0.go()
    if whole_heads:
        w_o = gather(clock.now(wo))
    else:
        w_o = lax.all_gather(clock.now(wo), ALL, axis=0, tiled=True)
        w_o = lax.dynamic_slice(w_o, (s * Dl, 0), (Dl, D))

    small = (gain_one, shift_one, bias_q, bias_v, bias_o, gain_two, shift_two, bias_out)
    packed = clock.did(gather_small(clock.now(jnp.concatenate(small + (bias_in,))), devices))
    full = lambda k: packed[:, k * r : (k + 1) * r].reshape(1, D).astype(f32)
    mine = lambda k: (
        lax.dynamic_index_in_dim(packed.reshape(B, S, -1), s, 1, False)[:, k * r : (k + 1) * r]
        if whole_heads
        else lax.dynamic_slice(packed[:, k * r : (k + 1) * r].reshape(D), (s * Dl,), (Dl,))
    ).reshape(Dl).astype(f32)
    gain_a, shift_a, bias_o_full, gain_b, shift_b, bias_out_full = (full(k) for k in (0, 1, 4, 5, 6, 7))
    bias_qkv = jnp.concatenate([mine(2), jnp.zeros((Dl,), f32), mine(3)])[None]
    bias_hidden = (
        lax.dynamic_index_in_dim(packed.reshape(B, S, -1), s, 1, False)[:, len(small) * r :]
        .reshape(1, Fl).astype(f32)
    )

    w_2 = gather(clock.now(w_out))
    in0.arrive()
    in1 = bring(inputs[1])
    start_layer(0, in0.result())
    in1.go()
    cot0 = bring(grad_two[0])
    attention(0)
    in1.arrive()
    br0 = begin(branch_out(0))
    w_1 = gather(clock.now(in_rows))
    start_layer(1, in1.result())
    cot0.go()
    attention(1)
    br0.go()
    part = branch_out(1)
    br0.arrive()
    nt0 = bring(middle_of(0, br0.result()))
    br1 = begin(part)
    cot0.arrive()
    grad_branch_two[0] = cot0.result()
    hidden_back(0)
    nt0.go()
    br1.go()
    cot1 = bring(grad_two[1])
    nt0.arrive()
    br1.arrive()
    nt1 = bring(middle_of(1, br1.result()))
    normed_two[0] = nt0.result()
    hidden_units(0)
    cot1.go()
    nt1.go()
    gn0 = begin(normed_two_back(0))
    cot1.arrive()
    grad_branch_two[1] = cot1.result()
    hidden_back(1)
    nt1.arrive()
    normed_two[1] = nt1.result()
    hidden_units(1)
    gn0.go()
    sum_w_2 = gradient(hidden, grad_branch_two)
    sum_w_2 = scatter(sum_w_2)
    part = branch_two_out(0)
    gn0.arrive()
    middle_back(0, gn0.result())
    gb0 = bring(own_grad_branch[0])
    gn1 = begin(normed_two_back(1))
    sum_w_1 = gradient(normed_two, grad_pre)
    gb0.go()
    gn1.go()
    part_one = branch_two_out(1)
    gb0.arrive()
    out0 = begin(part)
    grad_branch[0] = gb0.result()
    context_back(0)
    gn1.arrive()
    middle_back(1, gn1.result())
    gb1 = bring(own_grad_branch[1])
    sum_w_1 = scatter(after(clock.now(sum_w_1), sum_w_2))
    attention_back(0)
    gb1.go()
    part = normed_back(0)
    gb1.arrive()
    gx0 = begin(part)
    grad_branch[1] = gb1.result()
    context_back(1)
    out0.go()
    sum_o = gradient(context, grad_branch)
    out0.arrive()
    gx0.go()
    out1 = begin(part_one)
    attention_back(1)
    gx0.arrive()
    out1.go()
    sum_qkv = gradient(normed, grad_qkv)
    sum_qkv = scatter(after(clock.now(sum_qkv), sum_w_1))
    part = normed_back(1)
    out1.arrive()
    gx1 = begin(part)
    finish(0, out0.result())
    start_back(0, gx0.result())
    finish(1, out1.result())
    bias_sums = clock.did(tokens(clock.now(grad_qkv)))
    gx1.go()
    sum_w_1 = ring.swap(clock.now(sum_w_1).reshape(S, r, Fl))
    gx1.arrive()
    start_back(1, gx1.result())
    sum_w_1 = clock.did(unit_rows(clock.now(sum_w_1), B))
    sums = SmallScatter(clock, small_pack())
    for _ in range(3):
        sums.step()
    if whole_heads:
        sum_o = scatter(after(clock.now(sum_o), sum_qkv))
    else:
        sum_o = lax.dynamic_update_slice(jnp.zeros((D, D), bf16), sum_o, (s * Dl, 0))
        sum_o = lax.psum_scatter(after(clock.now(sum_o), sum_qkv), ALL, scatter_dimension=0, tiled=True)
    sum_qkv = ring.swap(clock.now(sum_qkv).reshape(S, r, 3 * Dl))
    sums = sums.result()
    if whole_heads:
        sum_q, sum_k, sum_v = head_rows(sum_qkv, B)
    else:
        sum_q, sum_k, sum_v = (
            sum_qkv[:, :, c * Dl : (c + 1) * Dl].transpose(1, 0, 2).reshape(r, D) for c in range(3)
        )

    g1, s1, bo, g2, s2, b2, bq, bv = (sums[k * r : (k + 1) * r] for k in range(8))
    wide = lambda v: v.astype(f32)
    return (
        output[-1], input_grad[-1], wide(sum_q), wide(sum_k), wide(sum_v), wide(sum_o),
        g1, s1, bq, bv, bo, sum_w_1, wide(sum_w_2), g2, s2, sums[8 * r :], b2,
    )


def solution(mesh):
    tokens, rows, vector = P("batch", "seq", None), P(ALL, None), P(ALL)
    placed = (
        (tokens, tokens, P("batch"), P("batch"), P())
        + (rows,) * 4 + (vector,) * 5 + (rows,) * 2 + (vector,) * 4
    )
    out = (tokens, tokens) + (rows,) * 4 + (vector,) * 5 + (rows,) * 2 + (vector,) * 4
    return jax.shard_map(body, mesh=mesh, in_specs=placed, out_specs=out, check_vma=False)
```

```python
from functools import partial

import jax
import jax.numpy as jnp
import numpy as np
from jax import lax
from jax.experimental import pallas as pl
from jax.experimental.pallas import tpu as pltpu
from jax.sharding import PartitionSpec as P

HEAD_DIM = 64
PAIR = 2 * HEAD_DIM
epsilon = 1e-05
LOG2E = 1.4426950408889634
bf16, f32 = jnp.bfloat16, jnp.float32
ALL = ("batch", "seq")
VMEM_LIMIT = 56 * 1024 * 1024


def dot_nn(a, b):
    return jnp.dot(a, b, preferred_element_type=f32)


def dot_nt(a, b):
    return lax.dot_general(a, b, (((1,), (1,)), ((), ())), preferred_element_type=f32)


def dot_tn(a, b):
    return lax.dot_general(a, b, (((0,), (0,)), ((), ())), preferred_element_type=f32)


PARAMS = pltpu.CompilerParams(vmem_limit_bytes=VMEM_LIMIT)
PACE = 0.5


def cost(flops):
    return pl.CostEstimate(flops=int(PACE * flops), bytes_accessed=int(PACE * flops / 320), transcendentals=0)


def tile_of(width, most=512):
    return next(t for t in (most, 256, 128, width) if width % t == 0)


def listed(value):
    return list(value) if isinstance(value, (list, tuple)) else [value]


def rows_of(pieces):
    return sum(p.shape[0] for p in pieces)


def fixed(shape):
    return pl.BlockSpec(shape, lambda j: (0,) * len(shape))


def join(refs, whole):
    at = 0
    for ref in refs:
        whole[at : at + ref.shape[0], :] = ref[...]
        at += ref.shape[0]


def first_step(body):
    pl.when(pl.program_id(0) == 0)(body)


def matmul(left, right, dot, parts=None):
    left = listed(left)
    n, rows, depth = len(left), rows_of(left), left[0].shape[1]
    width = right.shape[1] if dot is dot_nn else right.shape[0]
    tile, ranges = tile_of(width), parts or [[(0, rows)]]
    sizes = [sum(stop - begin for begin, stop in part) for part in ranges]

    def kernel(*refs):
        whole = refs[0]
        if n > 1:
            whole = refs[-1]
            first_step(lambda: join(refs[:n], whole))
        total = dot(whole[...], refs[n][...]).astype(bf16)
        for ref, part in zip(refs[n + 1 :], ranges):
            at = 0
            for begin, stop in part:
                ref[at : at + stop - begin, :] = total[begin:stop]
                at += stop - begin

    strip = (
        pl.BlockSpec((depth, tile), lambda j: (0, j)) if dot is dot_nn else pl.BlockSpec((tile, depth), lambda j: (j, 0))
    )
    out = pl.pallas_call(
        kernel,
        out_shape=tuple(jax.ShapeDtypeStruct((size, width), bf16) for size in sizes),
        grid=(width // tile,),
        in_specs=[fixed(p.shape) for p in left] + [strip],
        out_specs=tuple(pl.BlockSpec((size, tile), lambda j: (0, j)) for size in sizes),
        scratch_shapes=[pltpu.VMEM((rows, depth), bf16)] if n > 1 else [],
        compiler_params=PARAMS, cost_estimate=cost(3.5 * rows * depth * width), name="matmul",
    )(*left, right)
    return out if parts else out[0]


def weight_sum(lefts, rights):
    lefts, rights = [listed(v) for v in lefts], [listed(v) for v in rights]
    tokens = [rows_of(v) for v in lefts]
    rows, width = lefts[0][0].shape[1], rights[0][0].shape[1]
    tile = tile_of(rows, 256)
    sizes = [len(v) for v in lefts + rights]
    spots = [pltpu.VMEM((t, tile), bf16) for t in tokens] + [pltpu.VMEM((t, width), bf16) for t in tokens]
    spots = [spot if size > 1 else pltpu.VMEM((16, 128), bf16) for spot, size in zip(spots, sizes)]
    n = len(lefts)

    def kernel(*refs):
        out, spot, at, wholes = refs[sum(sizes)], refs[sum(sizes) + 1 :], 0, []
        for k, size in enumerate(sizes):
            group = refs[at : at + size]
            at += size
            if size == 1:
                wholes.append(group[0])
                continue
            wholes.append(spot[k])
            if k < n:
                join(group, spot[k])
            else:
                first_step(partial(join, group, spot[k]))
        total = sum(dot_tn(wholes[k][...], wholes[n + k][...]) for k in range(n))
        out[...] = total.astype(bf16)

    return pl.pallas_call(
        kernel,
        out_shape=jax.ShapeDtypeStruct((rows, width), bf16),
        grid=(rows // tile,),
        in_specs=[pl.BlockSpec((p.shape[0], tile), lambda j: (0, j)) for v in lefts for p in v]
        + [fixed(p.shape) for v in rights for p in v],
        out_specs=pl.BlockSpec((tile, width), lambda j: (j, 0)),
        scratch_shapes=spots,
        compiler_params=PARAMS, cost_estimate=cost(3.3 * sum(tokens) * rows * width), name="weight_sum",
    )(*(p for v in lefts + rights for p in v))


def norm_parts(rows):
    centered = rows - jnp.mean(rows, -1, keepdims=True)
    spread = jnp.mean(centered * centered, -1, keepdims=True)
    inverse = lax.rsqrt(spread + epsilon)
    return centered * inverse, inverse


def norm_back(grad, gain, unit, inverse):
    scaled = grad * gain
    return inverse * (
        scaled - jnp.mean(scaled, -1, keepdims=True) - unit * jnp.mean(scaled * unit, -1, keepdims=True)
    )


def project(pieces, gain, shift, w_qkv, bias):
    n, rows, (depth, width) = len(pieces), rows_of(pieces), w_qkv.shape
    tile = tile_of(width)

    def kernel(*refs):
        gain_ref, shift_ref, w_ref, bias_ref, normed, out = refs[n:]

        def norm():
            at = 0
            for ref in refs[:n]:
                for k in range(0, ref.shape[0], 64):
                    unit, _ = norm_parts(ref[k : k + 64, :].astype(f32))
                    normed[at + k : at + k + 64, :] = (unit * gain_ref[...] + shift_ref[...]).astype(bf16)
                at += ref.shape[0]

        first_step(norm)
        out[...] = (dot_nn(normed[...], w_ref[...]) + bias_ref[...]).astype(bf16)

    return pl.pallas_call(
        kernel,
        out_shape=(jax.ShapeDtypeStruct((rows, depth), bf16), jax.ShapeDtypeStruct((rows, width), bf16)),
        grid=(width // tile,),
        in_specs=[fixed(p.shape) for p in pieces]
        + [fixed((1, depth)), fixed((1, depth)), pl.BlockSpec((depth, tile), lambda j: (0, j)), pl.BlockSpec((1, tile), lambda j: (0, j))],
        out_specs=(fixed((rows, depth)), pl.BlockSpec((rows, tile), lambda j: (0, j))),
        compiler_params=PARAMS, cost_estimate=cost(5 * rows * depth * width), name="project",
    )(*pieces, gain, shift, w_qkv, bias)


def gelu_both(pre):
    below = 0.5 * (1.0 + lax.erf(pre * (0.5**0.5)))
    density = jnp.exp(-0.5 * pre * pre) * ((2.0 * np.pi) ** -0.5)
    return pre * below, below + pre * density


def hidden_both(normed, grad_hidden, w_1, bias):
    n, rows, (depth, width) = len(normed), rows_of(normed), w_1.shape
    tile = tile_of(width)

    def kernel(*refs):
        g_ref, w1_ref, b_ref, h_ref, p_ref, s_ref, whole = refs[n:]
        first_step(lambda: join(refs[:n], whole))
        value, slope = gelu_both(dot_nn(whole[...], w1_ref[...]) + b_ref[...])
        h_ref[...] = value.astype(bf16)
        grad_pre = (g_ref[...].astype(f32) * slope).astype(bf16)
        p_ref[...] = grad_pre
        s_ref[...] = jnp.sum(grad_pre.astype(f32), 0, keepdims=True)

    part = pl.BlockSpec((rows, tile), lambda j: (0, j))
    line = pl.BlockSpec((1, tile), lambda j: (0, j))
    return pl.pallas_call(
        kernel,
        out_shape=(jax.ShapeDtypeStruct((rows, width), bf16),) * 2 + (jax.ShapeDtypeStruct((1, width), f32),),
        grid=(width // tile,),
        in_specs=[fixed(p.shape) for p in normed] + [part, pl.BlockSpec((depth, tile), lambda j: (0, j)), line],
        out_specs=(part, part, line),
        scratch_shapes=[pltpu.VMEM((rows, depth), bf16)],
        compiler_params=PARAMS, cost_estimate=cost(5 * rows * depth * width), name="hidden_both",
    )(*normed, grad_hidden, w_1, bias)


STEP = 64


def own_rows(depth):
    return pl.BlockSpec((STEP, depth), lambda j: (j, 0))


def slot_rows(slot, depth):
    return pl.BlockSpec((1, STEP, depth), lambda j: (slot, j, 0))


def summed_rows(rows, depth):
    half = rows // 2 // STEP
    spec = lambda place: pl.BlockSpec((STEP, depth), lambda j: (place(j), 0))
    return [
        own_rows(depth), spec(lambda j: jnp.maximum(j, half)), spec(lambda j: jnp.minimum(j, half - 1) + half),
        spec(lambda j: jnp.minimum(j, half - 1)), spec(lambda j: jnp.maximum(j - half, 0)),
    ]


def summed(refs, steps):
    own, up, down, far_up, far_down = (ref[...].astype(f32) for ref in refs)
    early = pl.program_id(0) < steps // 2
    return own + jnp.where(early, far_up, up) + jnp.where(early, down, far_down)


def second_norm(slot, branch, inputs, active, bias, gain, shift):
    rows, depth = branch[0].shape

    def kernel(*refs):
        x, act, bias_ref, gain_ref, shift_ref, middle, normed = refs[5:]
        total = summed(refs[:5], rows // STEP) + bias_ref[...]
        total = x[0].astype(f32) + act[...] * total
        middle[...] = total
        normed[...] = (norm_parts(total)[0] * gain_ref[...] + shift_ref[...]).astype(bf16)

    return pl.pallas_call(
        kernel,
        out_shape=(jax.ShapeDtypeStruct((rows, depth), f32), jax.ShapeDtypeStruct((rows, depth), bf16)),
        grid=(rows // STEP,),
        in_specs=summed_rows(rows, depth) + [slot_rows(slot, depth), own_rows(1)] + [fixed((1, depth))] * 3,
        out_specs=(own_rows(depth), own_rows(depth)),
        compiler_params=PARAMS, cost_estimate=cost(6e9), name="second_norm",
    )(*branch, inputs, active, bias, gain, shift)


def add_line(sums, line, value):
    sums[line : line + 1, :] += jnp.sum(value, 0, keepdims=True)


def second_norm_back(slot, back, middle, cotangent, active, gain):
    rows, depth = middle.shape

    def kernel(*refs):
        mid, cot, act, gain_ref, grad_middle, grad_branch, sums = refs[5:]

        @first_step
        def _():
            sums[...] = jnp.zeros_like(sums)

        grad = summed(refs[:5], rows // STEP)
        unit, inverse = norm_parts(mid[...])
        outer = cot[0].astype(f32)
        total = outer + norm_back(grad, gain_ref[...], unit, inverse)
        grad_middle[...] = total
        branch = (act[...] * total).astype(bf16)
        grad_branch[...] = branch
        add_line(sums, 0, grad * unit)
        add_line(sums, 1, grad)
        add_line(sums, 2, branch.astype(f32))
        add_line(sums, 3, (act[...] * outer).astype(bf16).astype(f32))

    return pl.pallas_call(
        kernel,
        out_shape=(
            jax.ShapeDtypeStruct((rows, depth), f32), jax.ShapeDtypeStruct((rows, depth), bf16),
            jax.ShapeDtypeStruct((8, depth), f32),
        ),
        grid=(rows // STEP,),
        in_specs=summed_rows(rows, depth) + [own_rows(depth), slot_rows(slot, depth), own_rows(1), fixed((1, depth))],
        out_specs=(own_rows(depth), own_rows(depth), fixed((8, depth))),
        compiler_params=PARAMS, cost_estimate=cost(7e9), name="second_norm_back",
    )(*back, middle, cotangent, active, gain)


def first_norm_back(slot, back, inputs, grad_middle, gain, others):
    (rows, depth), slots = grad_middle.shape, inputs.shape[0]
    more = [] if others is None else [others]

    def kernel(*refs):
        x, grad_mid, gain_ref = refs[5:8]
        out, sums = refs[-2:]

        @first_step
        def _():
            sums[...] = jnp.zeros_like(sums)

        grad = summed(refs[:5], rows // STEP)
        unit, inverse = norm_parts(x[0].astype(f32))
        out[0] = (grad_mid[...] + norm_back(grad, gain_ref[...], unit, inverse)).astype(bf16)
        add_line(sums, 0, grad * unit)
        add_line(sums, 1, grad)

    return pl.pallas_call(
        kernel,
        out_shape=(jax.ShapeDtypeStruct((slots, rows, depth), bf16), jax.ShapeDtypeStruct((8, depth), f32)),
        grid=(rows // STEP,),
        in_specs=summed_rows(rows, depth) + [slot_rows(slot, depth), own_rows(depth), fixed((1, depth))]
        + [pl.BlockSpec(memory_space=pl.ANY)] * len(more),
        out_specs=(slot_rows(slot, depth), fixed((8, depth))),
        input_output_aliases={8: 0} if more else {},
        compiler_params=PARAMS, cost_estimate=cost(7e9), name="first_norm_back",
    )(*back, inputs, grad_middle, gain, *more)


def final_sum(slot, slots, branch, middle, active, bias, others):
    rows, depth = middle.shape
    more = [] if others is None else [others]

    def kernel(*refs):
        mid, act, bias_ref = refs[5:8]
        total = summed(refs[:5], rows // STEP) + bias_ref[...]
        refs[-1][0] = (mid[...] + act[...] * total).astype(bf16)

    return pl.pallas_call(
        kernel,
        out_shape=jax.ShapeDtypeStruct((slots, rows, depth), bf16),
        grid=(rows // STEP,),
        in_specs=summed_rows(rows, depth) + [own_rows(depth), own_rows(1), fixed((1, depth))] + [pl.BlockSpec(memory_space=pl.ANY)] * len(more),
        out_specs=slot_rows(slot, depth),
        input_output_aliases={8: 0} if more else {},
        compiler_params=PARAMS, cost_estimate=cost(6e9), name="final_sum",
    )(*branch, middle, active, bias, *more)


def head_pieces(weights, groups, blocks):
    rows = weights[0].shape[0]

    def kernel(*refs):
        for k in range(blocks):
            strips = [ref[:, (g * blocks + k) * rows : (g * blocks + k + 1) * rows] for ref in refs[:-1] for g in range(groups)]
            refs[-1][k] = jnp.concatenate(strips, 1)

    return pl.pallas_call(
        kernel,
        out_shape=jax.ShapeDtypeStruct((blocks, rows, 3 * groups * rows), bf16),
        compiler_params=PARAMS, cost_estimate=cost(2e9), name="head_pieces",
    )(*weights)


def unit_pieces(weight, groups, blocks):
    (rows, width), n = weight.shape, weight.shape[1] // (groups * blocks)

    def kernel(ref, out):
        for k in range(blocks):
            for g in range(groups):
                out[k, :, g * n : (g + 1) * n] = ref[:, (g * blocks + k) * n : (g * blocks + k + 1) * n]

    return pl.pallas_call(
        kernel,
        out_shape=jax.ShapeDtypeStruct((blocks, rows, groups * n), bf16),
        compiler_params=PARAMS, cost_estimate=cost(2e9), name="unit_pieces",
    )(weight) if n % 128 == 0 else weight.reshape(rows, groups, blocks, n).transpose(2, 0, 1, 3).reshape(blocks, rows, groups * n)


def unit_rows(pieces, groups):
    blocks, rows, width = pieces.shape
    n = width // groups

    def kernel(ref, out):
        for k in range(blocks):
            for g in range(groups):
                out[:, (g * blocks + k) * n : (g * blocks + k + 1) * n] = ref[k, :, g * n : (g + 1) * n].astype(f32)

    return pl.pallas_call(
        kernel,
        out_shape=jax.ShapeDtypeStruct((rows, blocks * width), f32),
        compiler_params=PARAMS, cost_estimate=cost(2e9), name="unit_rows",
    )(pieces) if n % 128 == 0 else pieces.reshape(blocks, rows, groups, n).transpose(1, 2, 0, 3).reshape(rows, -1).astype(f32)


def head_rows(pieces, groups):
    blocks, rows, width = pieces.shape

    def kernel(ref, *outs):
        for c, out in enumerate(outs):
            strips = [
                ref[k, :, (c * groups + g) * rows : (c * groups + g + 1) * rows] for g in range(groups) for k in range(blocks)
            ]
            out[...] = jnp.concatenate(strips, 1).astype(f32)

    return pl.pallas_call(
        kernel,
        out_shape=(jax.ShapeDtypeStruct((rows, blocks * width // 3), f32),) * 3,
        compiler_params=PARAMS, cost_estimate=cost(2e9), name="head_rows",
    )(pieces)


def after(value, others):
    return value if others is None else lax.optimization_barrier((value, others))[0]


class Clock:
    def __init__(self):
        self.last = None

    def now(self, value):
        return after(value, self.last)

    def did(self, value):
        self.last = jax.tree.leaves(value)
        return value


class Ring:
    def __init__(self, size):
        self.size = size
        self.order = [i ^ (i >> 1) for i in range(size)]
        self.place = [self.order.index(i) for i in range(size)]

    def parts(self, rows):
        n, half = self.size, rows // 2
        first = lambda k: (k * rows, k * rows + half)
        second = lambda k: (k * rows + half, (k + 1) * rows)
        far = n // 2
        out = [[(0, rows)], [first(far), second(far - 1)], [second(far), first(far + 1)]]
        for k in range(far - 1, 1, -1):
            out += [[first(k)], [second(k - 1)], [second(n - k)], [first(n - k + 1)]]
        return out + [[first(1)], [second(n - 1)]]

    def send(self, value, steps):
        n = self.size
        return lax.ppermute(value, "seq", [(self.order[i], self.order[(i + steps) % n]) for i in range(n)])

    def mine(self):
        place, shift = lax.axis_index("seq"), 1
        while shift < self.size:
            place = place ^ (place >> shift)
            shift *= 2
        return place

    def at(self, steps):
        place = (self.mine() + steps) & (self.size - 1)
        return place ^ (place >> 1)

    def steps_to(self):
        return (jnp.array(self.place, jnp.int32) - self.mine()) & (self.size - 1)

    def swap(self, pieces):
        take = lambda k: lax.dynamic_slice_in_dim(pieces, self.at(k), 1)
        out = lax.dynamic_update_slice_in_dim(jnp.zeros_like(pieces), take(0), self.at(0), 0)
        for k in range(1, self.size):
            came = self.send(take(k), k)
            out = lax.dynamic_update_slice_in_dim(out, came, self.at(-k), 0)
        return out


class Gather:
    def __init__(self, ring, clock, block):
        self.ring, self.clock = ring, clock
        self.half = block.shape[0] // 2
        self.near, self.far = [block], []
        block = clock.now(block)
        self.rising, self.falling = ring.send(block, 1), ring.send(block, -1)

    def go(self):
        ring = self.ring
        for _ in range(2, ring.size // 2):
            self.far.append(self.rising)
            self.near.append(self.falling)
            self.rising, self.falling = ring.send(self.rising, 1), ring.send(self.falling, -1)
        rising, falling = self.clock.did(self.clock.now((self.rising, self.falling)))
        self.far.append(rising)
        self.near.append(falling)
        first, second = self.clock.did((rising[: self.half], falling[self.half :]))
        self.middle = [ring.send(first, 1), ring.send(second, -1)]

    def arrive(self):
        self.middle = list(self.clock.did(self.clock.now(tuple(self.middle))))

    def result(self):
        return self.clock.now(self.near + self.middle + self.far[::-1])


class Scatter:
    def __init__(self, ring, clock, part):
        self.ring, self.clock, self.part = ring, clock, part
        self.up, self.down = ring.send(part[1], 1), ring.send(part[2], -1)

    def go(self):
        n, send, now, did = self.ring.size, self.ring.send, self.clock.now, self.clock.did
        half = self.part[1].shape[0] // 2
        rest = self.part[3:]
        for k in range(0, 4 * (n // 2 - 2), 4):
            up = jnp.concatenate([add16(rest[k], self.up[:half]), add16(rest[k + 1], self.up[half:])])
            down = jnp.concatenate([add16(rest[k + 2], self.down[:half]), add16(rest[k + 3], self.down[half:])])
            self.up, self.down = send(up, 1), send(down, -1)
        up, down = did(now((self.up, self.down)))
        far_up, far_down = did((add16(rest[-2], up[:half]), add16(rest[-1], down[:half])))
        self.up, self.down = up, down
        self.far_up, self.far_down = send(far_up, 1), send(far_down, -1)

    def arrive(self):
        self.far_up, self.far_down = self.clock.did(self.clock.now((self.far_up, self.far_down)))

    def result(self):
        return (self.part[0], self.up, self.down) + self.clock.now((self.far_up, self.far_down))


def add16(a, b):
    return (a.astype(f32) + b.astype(f32)).astype(bf16)


def gather_small(block, devices):
    place = lax.axis_index(ALL)
    have, bit = block[None], 1
    while bit < devices:
        other = lax.ppermute(have, ALL, [(i, i ^ bit) for i in range(devices)])
        low = (place & bit) == 0
        have = jnp.concatenate([jnp.where(low, have, other), jnp.where(low, other, have)])
        bit *= 2
    return have


class SmallScatter:
    def __init__(self, clock, total):
        self.clock, self.keep, self.came, self.devices = clock, total, None, total.shape[0]

    def gathered(self):
        total = self.clock.now(self.keep)
        return total if self.came is None else self.clock.did(total + self.clock.now(self.came))

    def step(self):
        bit = self.keep.shape[0] // 2
        if bit == 0:
            return
        total = self.gathered()
        low = (lax.axis_index(ALL) & bit) == 0
        self.keep = jnp.where(low, total[:bit], total[bit:])
        send = jnp.where(low, total[bit:], total[:bit])
        self.came = lax.ppermute(send, ALL, [(i, i ^ bit) for i in range(self.devices)])

    def result(self):
        while self.keep.shape[0] > 1:
            self.step()
        return self.gathered()[0]


def attend_kernel(blocks, rows, steps, q_ref, k_ref, v_ref, o_ref, lse_ref, keys, values_t):
    for a in range(blocks):
        here = pl.ds(pl.multiple_of(steps[a] * rows, rows), rows)
        keys[a * rows : (a + 1) * rows, :] = k_ref[here, :]
        values_t[:, a * rows : (a + 1) * rows] = v_ref[here, :].astype(f32).T.astype(bf16)
    lane = lax.broadcasted_iota(jnp.int32, (1, PAIR), 1)
    causal = lax.broadcasted_iota(jnp.int32, (rows, rows), 0) <= lax.broadcasted_iota(
        jnp.int32, (rows, rows), 1
    )
    scale = HEAD_DIM ** (-0.5) * LOG2E
    for i in range(blocks):
        here = pl.ds(pl.multiple_of(steps[i] * rows, rows), rows)
        query = q_ref[here, :]
        ahead = i * rows
        parts = []
        for head in range(2):
            own = (lane // HEAD_DIM == head).astype(bf16)
            lines = slice(head * HEAD_DIM, (head + 1) * HEAD_DIM)
            q_head = query * own
            diag = dot_nt(keys[ahead : ahead + rows, :], q_head) * scale
            diag = jnp.where(causal, diag, -1e30)
            top = jnp.max(diag, 0, keepdims=True)
            if i > 0:
                full = dot_nt(keys[:ahead, :], q_head) * scale
                top = jnp.maximum(top, jnp.max(full, 0, keepdims=True))
            diag = jnp.exp2(diag - top)
            total = jnp.sum(diag, 0, keepdims=True)
            mixed = dot_nn(values_t[lines, ahead : ahead + rows], diag.astype(bf16))
            if i > 0:
                full = jnp.exp2(full - top)
                total = total + jnp.sum(full, 0, keepdims=True)
                mixed = mixed + dot_nn(values_t[lines, :ahead], full.astype(bf16))
            parts.append(mixed / total)
            lse_ref[0, head : head + 1, ahead : ahead + rows] = top + jnp.log2(total)
        o_ref[here, :] = jnp.concatenate(parts).T.astype(bf16)


def attend(qkv, steps, blocks):
    tokens, width = qkv.shape[0], qkv.shape[1] // 3
    pairs, rows = width // PAIR, tokens // blocks
    column = lambda c: pl.BlockSpec((tokens, PAIR), lambda h, steps: (0, c * pairs + h))
    return pl.pallas_call(
        partial(attend_kernel, blocks, rows),
        out_shape=(
            jax.ShapeDtypeStruct((tokens, width), bf16),
            jax.ShapeDtypeStruct((pairs, 2, tokens), f32),
        ),
        grid_spec=pltpu.PrefetchScalarGridSpec(
            num_scalar_prefetch=1,
            grid=(pairs,),
            in_specs=[column(0), column(1), column(2)],
            out_specs=(column(0), pl.BlockSpec((1, 2, tokens), lambda h, steps: (h, 0, 0))),
            scratch_shapes=[pltpu.VMEM((tokens, PAIR), bf16), pltpu.VMEM((PAIR, tokens), bf16)],
        ),
        compiler_params=pltpu.CompilerParams(vmem_limit_bytes=VMEM_LIMIT),
        cost_estimate=cost(32 * tokens * tokens * width),
        name="attend",
    )(steps, qkv, qkv, qkv)


def attend_back_kernel(
    blocks, rows, steps, q_ref, k_ref, v_ref, g_ref, lse_ref, d_ref, keys, keys_t, values, dk, dv, dk16, dv16
):
    @pl.when(pl.program_id(1) == 0)
    def _():
        for a in range(blocks):
            here = pl.ds(pl.multiple_of(steps[a] * rows, rows), rows)
            place = slice(a * rows, (a + 1) * rows)
            keys[place, :] = k_ref[here, :]
            keys_t[:, place] = k_ref[here, :].astype(f32).T.astype(bf16)
            values[place, :] = v_ref[here, :]
        dk[...] = jnp.zeros_like(dk)
        dv[...] = jnp.zeros_like(dv)
        lane = lax.broadcasted_iota(jnp.int32, (1, PAIR), 1)
        scaling = HEAD_DIM ** (-0.5)
        for i in range(blocks):
            here = pl.ds(pl.multiple_of(steps[i] * rows, rows), rows)
            query, grad = q_ref[here, :], g_ref[here, :]
            length = (i + 1) * rows
            causal = lax.broadcasted_iota(jnp.int32, (length, rows), 0) <= (
                lax.broadcasted_iota(jnp.int32, (length, rows), 1) + i * rows
            )
            parts = []
            for head in range(2):
                own = (lane // HEAD_DIM == head).astype(bf16)
                lines = slice(head * HEAD_DIM, (head + 1) * HEAD_DIM)
                q_head, g_head = query * own, grad * own
                lse = lse_ref[0, head : head + 1, i * rows : (i + 1) * rows]
                logits = dot_nt(keys[:length, :], q_head) * (scaling * LOG2E)
                probs = jnp.where(causal, jnp.exp2(logits - lse), 0.0)
                grad_probs = dot_nt(values[:length, :], g_head)
                inner = jnp.sum(grad_probs * probs, 0, keepdims=True)
                grad_raw = (probs * (grad_probs - inner) * scaling).astype(bf16)
                parts.append(dot_nn(keys_t[lines, :length], grad_raw))
                dk[:length, :] += dot_nn(grad_raw, q_head)
                dv[:length, :] += dot_nn(probs.astype(bf16), g_head)
            d_ref[here, :] = jnp.concatenate(parts).T.astype(bf16)
        for a in range(blocks):
            here = pl.ds(pl.multiple_of(steps[a] * rows, rows), rows)
            dk16[here, :] = dk[a * rows : (a + 1) * rows, :].astype(bf16)
            dv16[here, :] = dv[a * rows : (a + 1) * rows, :].astype(bf16)

    @pl.when(pl.program_id(1) == 1)
    def _():
        d_ref[...] = dk16[...]

    @pl.when(pl.program_id(1) == 2)
    def _():
        d_ref[...] = dv16[...]


def attend_back(qkv, grad_context, lse, steps, blocks):
    tokens, width = grad_context.shape
    pairs, rows = width // PAIR, tokens // blocks
    column = lambda c: pl.BlockSpec((tokens, PAIR), lambda h, c_out, steps: (0, c * pairs + h))
    wide = lambda dtype: pltpu.VMEM((tokens, PAIR), dtype)
    return pl.pallas_call(
        partial(attend_back_kernel, blocks, rows),
        out_shape=jax.ShapeDtypeStruct((tokens, 3 * width), bf16),
        grid_spec=pltpu.PrefetchScalarGridSpec(
            num_scalar_prefetch=1,
            grid=(pairs, 3),
            in_specs=[
                column(0), column(1), column(2), column(0),
                pl.BlockSpec((1, 2, tokens), lambda h, c_out, steps: (h, 0, 0)),
            ],
            out_specs=pl.BlockSpec((tokens, PAIR), lambda h, c_out, steps: (0, c_out * pairs + h)),
            scratch_shapes=[
                wide(bf16), pltpu.VMEM((PAIR, tokens), bf16), wide(bf16),
                wide(f32), wide(f32), wide(bf16), wide(bf16),
            ],
        ),
        compiler_params=pltpu.CompilerParams(vmem_limit_bytes=VMEM_LIMIT),
        cost_estimate=cost(64 * tokens * tokens * width),
        name="attend_back",
    )(steps, qkv, qkv, qkv, grad_context, lse)


def body(
    inputs, cotangent, max_exit, min_exit, layer, wq, wk, wv, wo, gain_one, shift_one, bias_q, bias_v,
    bias_o, w_in, w_out, gain_two, shift_two, bias_in, bias_out,
):
    B, S = lax.axis_size("batch"), lax.axis_size("seq")
    devices = B * S
    s = lax.axis_index("seq")
    slots, T, D = inputs.shape
    r, rw = wq.shape[0], w_out.shape[0]
    Dl, Fl = D // S, rw * B
    whole_heads = r % HEAD_DIM == 0
    ring = Ring(S)
    steps = ring.steps_to()

    places = s * T + jnp.arange(T, dtype=jnp.int32)
    exits = max_exit[:, None] - (max_exit - min_exit)[:, None] * places[None, :] // (S * T - 1)
    active = (layer[0] < exits).astype(f32)[..., None]

    clock = Clock()
    grad_two = [(active[i] * cotangent[i].astype(f32)).astype(bf16) for i in range(slots)]
    gather = lambda x: lax.all_gather(x, "batch", axis=0, tiled=True)
    scatter = lambda x: lax.psum_scatter(x, "batch", scatter_dimension=0, tiled=True)
    qkv_pieces = (
        head_pieces((wq, wk, wv), B, S)
        if whole_heads
        else jnp.concatenate([w.reshape(r, S, Dl).transpose(1, 0, 2) for w in (wq, wk, wv)], -1)
    )
    in_pieces = unit_pieces(w_in, B, S)
    def start_layer(i, rows):
        normed[i], qkv[i] = clock.did(project(clock.now(rows), gain_a, shift_a, w_qkv, bias_qkv))

    def attention(i):
        context[i], lse[i] = clock.did(attend(clock.now(qkv[i]), steps, S))

    def branch_out(i):
        return clock.did(matmul(clock.now(context[i]), w_o, dot_nn, parts_out))

    def middle_of(i, branch):
        middle[i], own_normed = clock.did(
            second_norm(i, clock.now(branch), inputs, active[i], bias_o_full, gain_b, shift_b)
        )
        return own_normed

    def hidden_units(i):
        hidden[i], grad_pre[i], sum_pre[i] = clock.did(
            hidden_both(clock.now(normed_two[i]), grad_hidden[i], w_1, bias_hidden)
        )

    def hidden_back(i):
        grad_hidden[i] = clock.did(matmul(clock.now(grad_branch_two[i]), w_2, dot_nt))

    def normed_two_back(i):
        return clock.did(matmul(clock.now(grad_pre[i]), w_1, dot_nt, parts_out))

    def middle_back(i, back):
        grad_middle[i], own_grad_branch[i], sums_two[i] = clock.did(
            second_norm_back(i, clock.now(back), middle[i], cotangent, active[i], gain_b)
        )

    def context_back(i):
        grad_context[i] = clock.did(matmul(clock.now(grad_branch[i]), w_o, dot_nt))

    def attention_back(i):
        grad_qkv[i] = clock.did(attend_back(qkv[i], clock.now(grad_context[i]), lse[i], steps, S))

    def normed_back(i):
        return clock.did(matmul(clock.now(grad_qkv[i]), w_qkv, dot_nt, parts_out))

    def start_back(i, back):
        input_grad[i], sums_one[i] = clock.did(
            first_norm_back(i, clock.now(back), inputs, grad_middle[i], gain_a, input_grad[i - 1] if i else None)
        )

    def branch_two_out(i):
        return clock.did(matmul(clock.now(hidden[i]), w_2, dot_nn, parts_out))

    def finish(i, branch_two):
        output[i] = clock.did(
            final_sum(i, slots, clock.now(branch_two), middle[i], active[i], bias_out_full, output[i - 1] if i else None)
        )

    def gradient(lefts, rights):
        return clock.did(weight_sum(clock.now(lefts), rights))

    parts_out = ring.parts(T)

    tokens = lambda parts: sum(jnp.sum(p.astype(f32), 0) for p in parts)
    plain = lambda v: v.reshape(devices, r)
    pair_sum = lambda pairs, k: plain(pairs[0][k] + pairs[1][k])

    def own_heads(v):
        if whole_heads:
            spread = jnp.zeros((B, S, r), f32)
            return lax.dynamic_update_slice(spread, v.reshape(B, 1, r), (0, s, 0)).reshape(devices, r)
        return lax.dynamic_update_slice(jnp.zeros((D,), f32), v, (s * Dl,)).reshape(devices, r)

    def small_pack():
        own_hidden = lax.dynamic_update_slice(
            jnp.zeros((B, S, rw), f32), sum(sum_pre).reshape(B, 1, rw), (0, s, 0)
        ).reshape(devices, rw)
        parts = (
            pair_sum(sums_two, 2), pair_sum(sums_two, 0), pair_sum(sums_two, 1), pair_sum(sums_two, 3),
            own_heads(bias_sums[:Dl]), own_heads(bias_sums[2 * Dl :]), own_hidden,
        )
        last = pair_sum(sums_one, 0), pair_sum(sums_one, 1)
        return jnp.concatenate(last + parts, -1)

    fresh = lambda: [None] * slots
    normed, qkv, context, lse, middle, normed_two, sums_one, sums_two = (fresh() for _ in range(8))
    hidden, sum_pre, grad_pre, output, grad_middle, grad_branch = (fresh() for _ in range(6))
    own_grad_branch, grad_branch_two, grad_hidden, grad_context, grad_qkv, input_grad = (fresh() for _ in range(6))
    assert slots == 2
    begin, bring = partial(Scatter, ring, clock), partial(Gather, ring, clock)

    qkv_rows = clock.did(ring.swap(qkv_pieces).reshape(S * r, 3 * Dl))
    w_qkv = gather(qkv_rows)
    in_rows = ring.swap(clock.now(in_pieces)).reshape(S * r, Fl)
    in0 = bring(inputs[0])
    in_rows = clock.did(clock.now(in_rows))
    in0.go()
    if whole_heads:
        w_o = gather(clock.now(wo))
    else:
        w_o = lax.all_gather(clock.now(wo), ALL, axis=0, tiled=True)
        w_o = lax.dynamic_slice(w_o, (s * Dl, 0), (Dl, D))

    small = (gain_one, shift_one, bias_q, bias_v, bias_o, gain_two, shift_two, bias_out)
    packed = clock.did(gather_small(clock.now(jnp.concatenate(small + (bias_in,))), devices))
    full = lambda k: packed[:, k * r : (k + 1) * r].reshape(1, D).astype(f32)
    mine = lambda k: (
        lax.dynamic_index_in_dim(packed.reshape(B, S, -1), s, 1, False)[:, k * r : (k + 1) * r]
        if whole_heads
        else lax.dynamic_slice(packed[:, k * r : (k + 1) * r].reshape(D), (s * Dl,), (Dl,))
    ).reshape(Dl).astype(f32)
    gain_a, shift_a, bias_o_full, gain_b, shift_b, bias_out_full = (full(k) for k in (0, 1, 4, 5, 6, 7))
    bias_qkv = jnp.concatenate([mine(2), jnp.zeros((Dl,), f32), mine(3)])[None]
    bias_hidden = (
        lax.dynamic_index_in_dim(packed.reshape(B, S, -1), s, 1, False)[:, len(small) * r :]
        .reshape(1, Fl).astype(f32)
    )

    w_2 = gather(clock.now(w_out))
    in0.arrive()
    in1 = bring(inputs[1])
    start_layer(0, in0.result())
    in1.go()
    cot0 = bring(grad_two[0])
    attention(0)
    in1.arrive()
    br0 = begin(branch_out(0))
    w_1 = gather(clock.now(in_rows))
    start_layer(1, in1.result())
    cot0.go()
    attention(1)
    br0.go()
    part = branch_out(1)
    br0.arrive()
    nt0 = bring(middle_of(0, br0.result()))
    br1 = begin(part)
    cot0.arrive()
    grad_branch_two[0] = cot0.result()
    hidden_back(0)
    nt0.go()
    br1.go()
    cot1 = bring(grad_two[1])
    nt0.arrive()
    br1.arrive()
    nt1 = bring(middle_of(1, br1.result()))
    normed_two[0] = nt0.result()
    hidden_units(0)
    cot1.go()
    nt1.go()
    gn0 = begin(normed_two_back(0))
    cot1.arrive()
    grad_branch_two[1] = cot1.result()
    hidden_back(1)
    nt1.arrive()
    normed_two[1] = nt1.result()
    hidden_units(1)
    gn0.go()
    sum_w_2 = gradient(hidden, grad_branch_two)
    sum_w_2 = scatter(sum_w_2)
    part = branch_two_out(0)
    gn0.arrive()
    middle_back(0, gn0.result())
    gb0 = bring(own_grad_branch[0])
    gn1 = begin(normed_two_back(1))
    sum_w_1 = gradient(normed_two, grad_pre)
    gb0.go()
    gn1.go()
    part_one = branch_two_out(1)
    gb0.arrive()
    out0 = begin(part)
    grad_branch[0] = gb0.result()
    context_back(0)
    gn1.arrive()
    middle_back(1, gn1.result())
    gb1 = bring(own_grad_branch[1])
    sum_w_1 = scatter(after(clock.now(sum_w_1), sum_w_2))
    attention_back(0)
    gb1.go()
    part = normed_back(0)
    gb1.arrive()
    gx0 = begin(part)
    grad_branch[1] = gb1.result()
    context_back(1)
    sum_o = gradient(context, grad_branch)
    gx0.go()
    out0.go()
    attention_back(1)
    gx0.arrive()
    out0.arrive()
    out1 = begin(part_one)
    sum_qkv = gradient(normed, grad_qkv)
    out1.go()
    sum_qkv = scatter(after(clock.now(sum_qkv), sum_w_1))
    part = normed_back(1)
    out1.arrive()
    gx1 = begin(part)
    finish(0, out0.result())
    start_back(0, gx0.result())
    finish(1, out1.result())
    bias_sums = clock.did(tokens(clock.now(grad_qkv)))
    gx1.go()
    sum_w_1 = ring.swap(clock.now(sum_w_1).reshape(S, r, Fl))
    gx1.arrive()
    start_back(1, gx1.result())
    sum_w_1 = clock.did(unit_rows(clock.now(sum_w_1), B))
    sums = SmallScatter(clock, small_pack())
    for _ in range(3):
        sums.step()
    if whole_heads:
        sum_o = scatter(after(clock.now(sum_o), sum_qkv))
    else:
        sum_o = lax.dynamic_update_slice(jnp.zeros((D, D), bf16), sum_o, (s * Dl, 0))
        sum_o = lax.psum_scatter(after(clock.now(sum_o), sum_qkv), ALL, scatter_dimension=0, tiled=True)
    sum_qkv = ring.swap(clock.now(sum_qkv).reshape(S, r, 3 * Dl))
    sums = sums.result()
    if whole_heads:
        sum_q, sum_k, sum_v = head_rows(sum_qkv, B)
    else:
        sum_q, sum_k, sum_v = (
            sum_qkv[:, :, c * Dl : (c + 1) * Dl].transpose(1, 0, 2).reshape(r, D) for c in range(3)
        )

    g1, s1, bo, g2, s2, b2, bq, bv = (sums[k * r : (k + 1) * r] for k in range(8))
    wide = lambda v: v.astype(f32)
    return (
        output[-1], input_grad[-1], wide(sum_q), wide(sum_k), wide(sum_v), wide(sum_o),
        g1, s1, bq, bv, bo, sum_w_1, wide(sum_w_2), g2, s2, sums[8 * r :], b2,
    )


def solution(mesh):
    tokens, rows, vector = P("batch", "seq", None), P(ALL, None), P(ALL)
    placed = (
        (tokens, tokens, P("batch"), P("batch"), P())
        + (rows,) * 4 + (vector,) * 5 + (rows,) * 2 + (vector,) * 4
    )
    out = (tokens, tokens) + (rows,) * 4 + (vector,) * 5 + (rows,) * 2 + (vector,) * 4
    return jax.shard_map(body, mesh=mesh, in_specs=placed, out_specs=out, check_vma=False)
```
